32 devices in a mesh: req: 4 (over y, core), tp: 8 (over z, x).
Axes of the slice: x: 2, y: 2, z: 4, core: 2. Of those that a mesh axis runs over, the one named last changes fastest.
Arguments:
- patches: bfloat16 [4, 512, 1664], P('req', 'tp'), may hold values from -6 to 6
- vis_gain: float32 [1664], replicated, may hold values from 0.1 to 1.9
- w_fc1: bfloat16 [1664, 8192], P(None, 'tp'), may hold values from -0.15625 to 0.15625
- w_fc2: bfloat16 [8192, 1664], P('tp'), may hold values from -0.125 to 0.125
- merge_gain: float32 [1664], replicated, may hold values from 0.1 to 1.9
- w_merge: bfloat16 [6656, 1664], P('tp'), may hold values from -0.078125 to 0.078125
- slots: int32 [4, 128], P('req'), may hold values from 0 to 1535, as said below
- text: bfloat16 [4, 1536, 1664], P('req', 'tp'), may hold values from -6 to 6
- docs: int32 [4, 1536], P('req'), may hold values from 0 to 7, never falling along the last dimension, each value on 1 to 384 neighbouring positions
- dec_gain: float32 [1664], replicated, may hold values from 0.1 to 1.9
- w_qkv: bfloat16 [1664, 4992], P(None, 'tp'), may hold values from -0.2773501 to 0.2773501
- w_out: bfloat16 [1664, 1664], P('tp'), may hold values from -0.625 to 0.625
Outputs:
- decoded: bfloat16 [4, 1536, 1664], P('req', 'tp')
The draws below stay inside these ranges and needn't reach their ends.
Inputs may be any that keep to these rules, and one draw needn't show every extreme that they name: `slots`: positions in a group are distinct; each image's 64 merged rows take consecutive positions in order, and image k lies within positions j * 768 to (j + 1) * 768 - 1 with j = (k + 1) mod 2; the image with j = 1 takes the last 64 positions of the prompt. `docs`: request numbers never fall along a prompt; each request spans 1 to 384 positions.
All inputs are finite; a program needn't handle non-finite values.
Results may differ from the reference program's by a relative error of at most 0.033.
Values may be sent and summed in bfloat16 or wider, within the bound.
No kernel may reach another device: no remote copies, remote signals or barrier semaphores. Data moves between devices by JAX's collectives and lax.ppermute only.
A program may use at most 64 MiB of HBM per device.

```python
import math
import jax
import jax.numpy as jnp
import numpy as np
from jax import lax

VD = 1664
FF = 8192
D = 1664
HEADS = 16
HD = 104
IMG_ROWS = 64
DOCS = 8
GROUPS = 4
PATCH = 512
MGRP = 128
SEQ = 1536
IMAGES = 2
N_TP = 8


def draw_slots(key, part):
    span = SEQ // IMAGES
    image_ids = jnp.arange(IMAGES, dtype=jnp.int32)
    target = (image_ids + IMAGES // 2) % IMAGES
    random_starts = jax.random.randint(key, (GROUPS, IMAGES), 0, span - IMG_ROWS + 1)
    final_span = (target == IMAGES - 1)[None, :]
    starts = jnp.where(final_span, span - IMG_ROWS, random_starts) + target[None, :] * span
    rows = starts[:, :, None] + jnp.arange(IMG_ROWS, dtype=jnp.int32)[None, None, :]
    return rows.reshape(GROUPS, MGRP).astype(jnp.int32)


def draw_text(key, part):
    values = jax.random.truncated_normal(jax.random.fold_in(key, 21), -6.0, 6.0, (GROUPS, SEQ, D), jnp.float32)
    return values.astype(jnp.bfloat16)


def draw_w_qkv(key, part):
    spread = (D // 2) ** (-0.5)
    values = jax.random.truncated_normal(jax.random.fold_in(key, 31), -6.0, 6.0, (D, 3 * D), jnp.float32) * spread
    return values.astype(jnp.bfloat16)


def levels(rng, shape, shards, smallest, high):
    level, own = 1.0, jax.random.fold_in(rng, 6)
    for dim, blocks in shards:
        heights = jnp.exp(jax.random.uniform(jax.random.fold_in(own, dim), (blocks,), jnp.float32, smallest / len(shards), high / len(shards)))
        level = level * jnp.repeat(heights, shape[dim] // blocks).reshape([-1 if axis == dim else 1 for axis in range(len(shape))])
    return level


def profile(count, total, bound, slope):
    portions = [(1 << 20) // math.isqrt(rank ** slope) + 1 for rank in range(2, count + 1)]
    rest, given = total - bound - (count - 1), [1] * (count - 1)
    while rest > 0:
        candidates = [i for i in range(count - 1) if given[i] < bound]
        whole, left = sum([portions[i] for i in candidates]), rest
        for i in candidates:
            extra = min(bound - given[i], max(1, left * portions[i] // whole), rest)
            given[i] = given[i] + extra
            rest = rest - extra
    return np.array([bound] + given)


def uneven(rng, count, total, reach, lean):
    if count == 2:
        one = jax.random.randint(rng, (), max(1, total - reach), min(reach, total - 1) + 1)
        return jnp.stack([one, total - one])
    lengths = jnp.asarray(profile(count, total, reach, lean), jnp.int32)
    couples = (count - 1) // 2
    giver, receiver = lengths[1:1 + 2 * couples:2], lengths[2:2 + 2 * couples:2]
    margin = jnp.minimum(giver - 1, reach - receiver)
    moved = jax.random.randint(jax.random.fold_in(rng, 1), (couples,), 0, 1 << 20) % (margin + 1)
    lengths = lengths.at[1:1 + 2 * couples:2].set(giver - moved).at[2:2 + 2 * couples:2].set(receiver + moved)
    return lengths[jax.random.permutation(jax.random.fold_in(rng, 2), count)]


def bell_draw(stream_key, extent, deviation, bound, shards=(), held_as=jnp.bfloat16):
    entries = jax.random.normal(stream_key, extent, jnp.float32) * deviation
    if len(shards) > 0:
        entries = levels(stream_key, extent, shards, -0.22, 0.18) * entries
    return jnp.clip(entries, min=-bound, max=bound).astype(held_as)


def setup_inputs(seed: int = 0) -> dict:
    streams_of = jax.random.split(jax.random.key(seed), 13)
    return {
        "patches": bell_draw(streams_of[0], (GROUPS, PATCH, VD), 1.0, 6.0, ((0, 4), (1, 8))),
        "vis_gain": jnp.clip(1.0 + 0.18 * jax.random.normal(streams_of[1], (VD,), jnp.float32), 0.1, 1.9),
        "w_fc1": bell_draw(streams_of[2], (VD, FF), VD ** -0.5, 0.15625, ((1, 8),)),
        "w_fc2": bell_draw(streams_of[3], (FF, VD), (FF // 4) ** -0.5, 0.125, ((0, 8),)),
        "merge_gain": jnp.clip(1.0 + 0.18 * jax.random.normal(streams_of[4], (VD,), jnp.float32), 0.1, 1.9),
        "w_merge": bell_draw(streams_of[5], (4 * VD, D), (4 * VD) ** -0.5, 0.078125, ((0, 8),)),
        "slots": draw_slots(jax.random.fold_in(streams_of[12], 71), 0),
        "text": draw_text(jax.random.fold_in(streams_of[12], 71), 0),
        "docs": jax.vmap(lambda own: jnp.searchsorted(jnp.cumsum(uneven(own, DOCS, SEQ, SEQ // 4, 2)), jnp.arange(SEQ), side="right"))(jax.random.split(streams_of[8], GROUPS)).reshape((GROUPS, SEQ)).astype(jnp.int32),
        "dec_gain": jnp.clip(1.0 + 0.18 * jax.random.normal(streams_of[9], (D,), jnp.float32), 0.1, 1.9),
        "w_qkv": draw_w_qkv(jax.random.fold_in(streams_of[12], 71), 0),
        "w_out": bell_draw(streams_of[11], (D, D), HD ** -0.5, 0.625, ((0, 8),)),
    }


EPSILON = 1e-06

def layer_norm(values, gains):
    average = lax.optimization_barrier(jnp.mean(values, axis=-1, keepdims=True))
    centred = values - average
    variance = lax.optimization_barrier(jnp.mean(centred * centred, axis=-1, keepdims=True))
    return centred * lax.rsqrt(variance + EPSILON) * gains

def rms_norm(values, gains):
    return values * lax.rsqrt(lax.optimization_barrier(jnp.mean(values * values, axis=-1, keepdims=True)) + EPSILON) * gains

def rounded_sum(parts):
    narrow = lax.optimization_barrier(parts.astype(jnp.bfloat16))
    return lax.optimization_barrier(jnp.sum(narrow.astype(jnp.float32), axis=0))

def reference(patches, vis_gain, w_fc1, w_fc2, merge_gain, w_merge, slots, text, docs, dec_gain, w_qkv, w_out):
    block_rows = min(512, SEQ)

    def one_group(packed):
        patch_rows, slot_row, text_rows, doc_row = packed
        wide_in = patch_rows.astype(jnp.float32)
        normed_in = layer_norm(wide_in, vis_gain.astype(jnp.float32)).astype(jnp.bfloat16)
        hidden = jax.nn.gelu(jnp.dot(normed_in, w_fc1, preferred_element_type=jnp.float32), approximate=False).astype(jnp.bfloat16)
        mlp_parts = jnp.einsum('pjh,jhv->jpv', hidden.reshape(PATCH, N_TP, FF // N_TP).astype(jnp.float32), w_fc2.reshape(N_TP, FF // N_TP, VD).astype(jnp.float32))
        mlp_sum = rounded_sum(mlp_parts)
        normed_out = layer_norm(wide_in + mlp_sum, merge_gain.astype(jnp.float32)).astype(jnp.bfloat16)
        merge_in = normed_out.reshape(MGRP, 4 * VD)
        merge_parts = jnp.einsum('mjf,jfd->jmd', merge_in.reshape(MGRP, N_TP, 4 * VD // N_TP).astype(jnp.float32), w_merge.reshape(N_TP, 4 * VD // N_TP, D).astype(jnp.float32))
        merged = rounded_sum(merge_parts).astype(jnp.bfloat16)
        embedded = text_rows.at[slot_row].set(merged)
        dec_in = rms_norm(embedded.astype(jnp.float32), dec_gain.astype(jnp.float32)).astype(jnp.bfloat16)
        qkv = jnp.dot(dec_in, w_qkv, preferred_element_type=jnp.float32).astype(jnp.bfloat16)
        shaped = qkv.reshape(SEQ, HEADS, 3, HD).astype(jnp.float32)
        queries = shaped[:, :, 0]
        key_rows = shaped[:, :, 1]
        value_rows = shaped[:, :, 2]
        key_pos = jnp.arange(SEQ)

        def one_block(block_index):
            offset = block_index * block_rows
            query_block = lax.dynamic_slice_in_dim(queries, offset, block_rows, 0)
            query_pos = offset + jnp.arange(block_rows)
            query_docs = lax.dynamic_slice_in_dim(doc_row, offset, block_rows, 0)
            scores = jnp.einsum('qhe,khe->hqk', query_block, key_rows) / math.sqrt(HD)
            allowed = (key_pos[None, :] <= query_pos[:, None]) & (doc_row[None, :] == query_docs[:, None])
            scores = jnp.where(allowed[None], scores, -1e+30)
            largest = lax.optimization_barrier(jnp.max(scores, axis=-1, keepdims=True))
            raised = jnp.where(allowed[None], jnp.exp(scores - largest), 0.0)
            weights = (raised / lax.optimization_barrier(jnp.sum(raised, axis=-1, keepdims=True))).astype(jnp.bfloat16)
            blended = jnp.einsum('hqk,khe->qhe', weights.astype(jnp.float32), value_rows)
            return blended.astype(jnp.bfloat16).reshape(block_rows, D)
        attended = lax.map(one_block, jnp.arange(SEQ // block_rows)).reshape(SEQ, D)
        out_parts = jnp.einsum('sjc,jcd->jsd', attended.reshape(SEQ, N_TP, D // N_TP).astype(jnp.float32), w_out.reshape(N_TP, D // N_TP, D).astype(jnp.float32))
        out_sum = rounded_sum(out_parts)
        return (embedded.astype(jnp.float32) + out_sum).astype(jnp.bfloat16)
    return lax.map(one_group, (patches, slots, text, docs))
```

```python
import math

import jax
import jax.numpy as jnp
from jax import lax
from jax.sharding import PartitionSpec as P

HD = 104


EPSILON = 1e-06


def layer_norm(values, gains):
    average = jnp.mean(values, axis=-1, keepdims=True)
    centred = values - average
    variance = jnp.mean(centred * centred, axis=-1, keepdims=True)
    return centred * lax.rsqrt(variance + EPSILON) * gains


def rms_norm(values, gains):
    return values * lax.rsqrt(jnp.mean(values * values, axis=-1, keepdims=True) + EPSILON) * gains


def attend(qkv_rows, doc_row, heads_here):
    seq_len = qkv_rows.shape[0]
    block_rows = min(512, seq_len)
    shaped = qkv_rows.reshape(seq_len, heads_here, 3, HD)
    queries = shaped[:, :, 0]
    key_rows = shaped[:, :, 1]
    value_rows = shaped[:, :, 2]
    key_pos = jnp.arange(seq_len)

    def one_block(block_index):
        offset = block_index * block_rows
        query_block = lax.dynamic_slice_in_dim(queries, offset, block_rows, 0)
        query_pos = offset + jnp.arange(block_rows)
        query_docs = lax.dynamic_slice_in_dim(doc_row, offset, block_rows, 0)
        scores = jnp.einsum(
            "qhe,khe->hqk", query_block, key_rows, preferred_element_type=jnp.float32
        ) / math.sqrt(HD)
        allowed = (key_pos[None, :] <= query_pos[:, None]) & (
            doc_row[None, :] == query_docs[:, None]
        )
        scores = jnp.where(allowed[None], scores, -1e30)
        largest = jnp.max(scores, axis=-1, keepdims=True)
        raised = jnp.where(allowed[None], jnp.exp(scores - largest), 0.0)
        weights = (raised / jnp.sum(raised, axis=-1, keepdims=True)).astype(jnp.bfloat16)
        blended = jnp.einsum(
            "hqk,khe->qhe", weights, value_rows, preferred_element_type=jnp.float32
        )
        return blended.astype(jnp.bfloat16).reshape(block_rows, heads_here * HD)

    blocks = lax.map(one_block, jnp.arange(seq_len // block_rows))
    return blocks.reshape(seq_len, heads_here * HD)


def pair_steps(tp_size):
    return [(i, i ^ 1) for i in range(tp_size)]


def turn_steps(tp_size, turn):
    lines = tp_size // 2
    return [(a * 2 + b, ((a + turn) % lines) * 2 + b) for a in range(lines) for b in range(2)]


def swap_pair(values, tp_size):
    return lax.ppermute(values, "tp", pair_steps(tp_size))


def turned(values, tp_size, turn):
    return lax.ppermute(values, "tp", turn_steps(tp_size, turn))


def shards(
    patches, vis_gain, w_fc1, w_fc2, merge_gain, w_merge, slots, text, docs, dec_gain, w_qkv, w_out
):
    patch_rows = patches[0]
    slot_row = slots[0]
    text_rows = text[0]
    doc_row = docs[0]
    width = patch_rows.shape[1]
    local_rows = patch_rows.shape[0]
    seq_here = text_rows.shape[0]
    wide_in = patch_rows.astype(jnp.float32)
    tp_size = lax.axis_size("tp")
    lines = tp_size // 2
    line = lax.axis_index("tp") // 2
    side = lax.axis_index("tp") % 2
    mine = [patch_rows] + [turned(patch_rows, tp_size, k) for k in range(1, lines)]
    other = [swap_pair(block, tp_size) for block in mine]
    rows = jnp.concatenate([part for k in range(lines) for part in (mine[k], other[k])], axis=0)
    normed_in = layer_norm(rows.astype(jnp.float32), vis_gain).astype(jnp.bfloat16)
    hidden = jax.nn.gelu(
        jnp.dot(normed_in, w_fc1, preferred_element_type=jnp.float32), approximate=False
    ).astype(jnp.bfloat16)
    part = jnp.dot(hidden, w_fc2, preferred_element_type=jnp.float32).astype(jnp.bfloat16)
    part = part.reshape(lines, 2, local_rows, width)
    mlp_sum = jnp.zeros((local_rows, width), jnp.float32)
    for k in range(lines):
        pair = part[k, 0].astype(jnp.float32) + swap_pair(part[k, 1], tp_size).astype(jnp.float32)
        if k:
            pair = turned(pair.astype(jnp.bfloat16), tp_size, lines - k).astype(jnp.float32)
        mlp_sum = mlp_sum + pair
    normed_out = layer_norm(wide_in + mlp_sum, merge_gain).astype(jnp.bfloat16)
    quads = local_rows // 4
    blocks = normed_out.reshape(quads, lines, 2, 4 * width // tp_size)
    kept = lax.dynamic_index_in_dim(blocks, side, 2, keepdims=False)
    given = swap_pair(lax.dynamic_index_in_dim(blocks, 1 - side, 2, keepdims=False), tp_size)
    both = jnp.where(side == 0, jnp.stack([kept, given]), jnp.stack([given, kept]))
    features = jnp.zeros((lines, 2, quads, both.shape[3]), jnp.bfloat16)
    for k in range(lines):
        target = (line + k) % lines
        block = lax.dynamic_index_in_dim(both, target, 2, keepdims=False)
        if k:
            block = turned(block, tp_size, k)
        source = (line + lines - k) % lines
        features = lax.dynamic_update_index_in_dim(features, block, source, 0)
    features = features.reshape(lines * 2 * quads, both.shape[3])
    merge_term = jnp.dot(features, w_merge, preferred_element_type=jnp.float32)
    half = merge_term.shape[1] // 2
    low, high = merge_term[:, :half], merge_term[:, half:]
    sent = jnp.where(side == 0, high, low).astype(jnp.bfloat16)
    summed = jnp.where(side == 0, low, high) + swap_pair(sent, tp_size).astype(jnp.float32)
    share = summed.reshape(lines, -1, half).astype(jnp.bfloat16)
    total = lax.dynamic_index_in_dim(share, line, 0, keepdims=False).astype(jnp.float32)
    for k in range(1, lines):
        block = lax.dynamic_index_in_dim(share, (line + k) % lines, 0, keepdims=False)
        total = total + turned(block, tp_size, k).astype(jnp.float32)
    total = total.astype(jnp.bfloat16)
    gathered = jnp.zeros((lines,) + total.shape, jnp.bfloat16)
    for k in range(lines):
        block = turned(total, tp_size, k) if k else total
        gathered = lax.dynamic_update_index_in_dim(gathered, block, (line + lines - k) % lines, 0)
    gathered = gathered.reshape(-1, half)
    far = swap_pair(gathered, tp_size)
    merged = jnp.where(
        side == 0,
        jnp.concatenate([gathered, far], axis=1),
        jnp.concatenate([far, gathered], axis=1),
    )
    positions = lax.axis_index("tp") * seq_here + jnp.arange(seq_here, dtype=jnp.int32)
    matches = slot_row[None, :] == positions[:, None]
    placed = jnp.dot(
        matches.astype(jnp.bfloat16), merged, preferred_element_type=jnp.float32
    ).astype(jnp.bfloat16)
    embedded = jnp.where(jnp.any(matches, axis=1)[:, None], placed, text_rows)
    dec_in = rms_norm(embedded.astype(jnp.float32), dec_gain).astype(jnp.bfloat16)
    qkv_rows = jnp.dot(
        lax.all_gather(dec_in, "tp", axis=0, tiled=True), w_qkv, preferred_element_type=jnp.float32
    ).astype(jnp.bfloat16)
    heads_here = qkv_rows.shape[1] // (3 * HD)
    attended = attend(qkv_rows, doc_row, heads_here)
    out_sum = lax.psum_scatter(
        jnp.dot(attended, w_out, preferred_element_type=jnp.float32).astype(jnp.bfloat16),
        "tp",
        scatter_dimension=0,
        tiled=True,
    ).astype(jnp.float32)
    decoded = (embedded.astype(jnp.float32) + out_sum).astype(jnp.bfloat16)
    return decoded[None]


def solution(mesh):
    placed = (
        P("req", "tp", None),
        P(),
        P(None, "tp"),
        P("tp", None),
        P(),
        P("tp", None),
        P("req", None),
        P("req", "tp", None),
        P("req", None),
        P(),
        P(None, "tp"),
        P("tp", None),
    )
    return jax.shard_map(
        shards, mesh=mesh, in_specs=placed, out_specs=P("req", "tp", None), check_vma=False
    )
```

```python
import functools
import math

import jax
import jax.numpy as jnp
from jax import lax
from jax.experimental import pallas as pl
from jax.experimental.pallas import tpu as pltpu
from jax.sharding import PartitionSpec as P

HD = 104


EPSILON = 1e-06


def layer_norm(values, gains):
    average = jnp.mean(values, axis=-1, keepdims=True)
    centred = values - average
    variance = jnp.mean(centred * centred, axis=-1, keepdims=True)
    return centred * lax.rsqrt(variance + EPSILON) * gains


def rms_norm(values, gains):
    return values * lax.rsqrt(jnp.mean(values * values, axis=-1, keepdims=True) + EPSILON) * gains


def pair_steps(tp_size):
    return [(i, i ^ 1) for i in range(tp_size)]


def turn_steps(tp_size, turn):
    lines = tp_size // 2
    return [(a * 2 + b, ((a + turn) % lines) * 2 + b) for a in range(lines) for b in range(2)]


def swap_pair(values, tp_size):
    return lax.ppermute(values, "tp", pair_steps(tp_size))


def turned(values, tp_size, turn):
    return lax.ppermute(values, "tp", turn_steps(tp_size, turn))


NT = (((1,), (1,)), ((), ()))
TN = (((0,), (0,)), ((), ()))


def put_quarters(whole, own, ours, theirs, starts, offset):
    step = pl.program_id(0)

    @pl.when(step == 0)
    def _():
        whole[...] = own[...]

    @pl.when(step > 0)
    def _():
        size = ours.shape[2]
        for index in range(4):
            quarter = ours[index // 2, 0] if index % 2 == 0 else theirs[index // 2, 0]
            start = pl.multiple_of(starts[offset + index], 16)
            whole[pl.ds(start, size), :] = quarter


def text_kernel(starts, rows, own, ours, theirs, out, whole):
    put_quarters(whole, own, ours, theirs, starts, 0)
    out[0] = lax.dot_general(
        whole[...], rows[...], NT, preferred_element_type=jnp.float32
    ).astype(jnp.bfloat16)


def late_kernel(
    blk, longest, starts, merged, gain, slots, key_docs, query_docs, text_part,
    own, ours, theirs, own_out, ours_out, theirs_out,
    out, whole, whole_out, image_rows, spread, hits, bias, total,
):
    step = pl.program_id(0)
    window = text_part.shape[2]
    ahead = window - blk
    reach = longest + 128
    shift = ahead - longest

    @pl.when(step == 0)
    def _():
        wide = merged[...].astype(jnp.float32)
        scale = lax.rsqrt(jnp.mean(wide * wide, axis=-1, keepdims=True) + EPSILON)
        image_rows[...] = (wide * scale * gain[...]).astype(jnp.bfloat16)
        position = starts[8] + lax.broadcasted_iota(jnp.int32, spread.shape, 1)
        match = jnp.where(slots[...] == position, 1.0, 0.0)
        spread[...] = match.astype(jnp.bfloat16)
        hits[...] = jnp.broadcast_to(jnp.max(match, axis=0, keepdims=True), hits.shape)
        for block in range(blk // 128):
            first = shift + block * 128
            key_place = first + lax.broadcasted_iota(jnp.int32, (reach, 128), 0)
            query_place = ahead + block * 128 + lax.broadcasted_iota(jnp.int32, (reach, 128), 1)
            allowed = (key_place <= query_place) & (
                key_docs[pl.ds(first, reach), :] == query_docs[:, pl.ds(block * 128, 128)]
            )
            bias[block] = jnp.where(allowed, 0.0, -1e30)
        total[...] = jnp.zeros_like(total)

    put_quarters(whole, own, ours, theirs, starts, 0)
    put_quarters(whole_out, own_out, ours_out, theirs_out, starts, 4)
    image_part = lax.dot_general(
        whole[...], image_rows[...], NT, preferred_element_type=jnp.float32
    ).astype(jnp.bfloat16)
    placed = jnp.dot(image_part, spread[...], preferred_element_type=jnp.float32)
    qkv = jnp.where(hits[0:1, :] > 0.5, placed, text_part[0].astype(jnp.float32))
    factor = math.log2(math.e) / math.sqrt(HD)
    heads = []
    for head in range(qkv.shape[0] // (3 * HD)):
        base = head * 3 * HD
        queries = (qkv[base : base + HD, ahead:] * factor).astype(jnp.bfloat16)
        keys = qkv[base + HD : base + 2 * HD].T.astype(jnp.bfloat16)
        values = qkv[base + 2 * HD : base + 3 * HD].astype(jnp.bfloat16)
        blocks = []
        for block in range(blk // 128):
            first = shift + block * 128
            scores = jnp.dot(
                keys[first : first + reach],
                queries[:, block * 128 : block * 128 + 128],
                preferred_element_type=jnp.float32,
            ) + bias[block]
            raised = jnp.exp2(scores - jnp.max(scores, axis=0, keepdims=True))
            blended = jnp.dot(
                values[:, first : first + reach],
                raised.astype(jnp.bfloat16),
                preferred_element_type=jnp.float32,
            )
            blocks.append(blended / jnp.sum(raised, axis=0, keepdims=True))
        heads.append(jnp.concatenate(blocks, axis=1))
    attended = jnp.concatenate(heads, axis=0).T.astype(jnp.bfloat16)
    depth = attended.shape[1]
    total[...] += jnp.dot(attended, whole_out[:depth], preferred_element_type=jnp.float32)

    @pl.when(step == pl.num_programs(0) - 1)
    def _():
        out[...] = total[...].astype(jnp.bfloat16)


def quarter_size(rows):
    return -(-rows // 64) * 16


def quarter_start(rows, index):
    return jnp.minimum(index * quarter_size(rows), rows - quarter_size(rows))


def gather_lines(weights, tp_size, first_after):
    lines = tp_size // 2
    copies = lax.axis_size("req")
    weights = jnp.pad(weights, ((0, -weights.shape[0] % 16), (0, 0)))
    place = lax.axis_index("req") % 4
    size = quarter_size(weights.shape[0])
    quarter = lax.dynamic_slice_in_dim(weights, quarter_start(weights.shape[0], place), size, 0)
    quarter = lax.optimization_barrier((quarter, first_after))[0]
    near = jnp.stack([turned(quarter, tp_size, k) for k in range(1, lines)])
    far = lax.ppermute(near, "req", [(i, i ^ 2) for i in range(copies)])
    ours = jnp.stack([near, far])
    theirs = lax.ppermute(ours, "req", [(i, i ^ 1) for i in range(copies)])
    return weights, ours, theirs


def shards(
    patches, vis_gain, w_fc1, w_fc2, merge_gain, w_merge, slots, text, docs, dec_gain, w_qkv, w_out
):
    patch_rows = patches[0]
    slot_row = slots[0]
    text_rows = text[0]
    doc_row = docs[0]
    width = patch_rows.shape[1]
    local_rows = patch_rows.shape[0]
    seq_here = text_rows.shape[0]
    wide_in = patch_rows.astype(jnp.float32)
    tp_size = lax.axis_size("tp")
    lines = tp_size // 2
    line = lax.axis_index("tp") // 2
    side = lax.axis_index("tp") % 2
    mine = [patch_rows] + [turned(patch_rows, tp_size, k) for k in range(1, lines)]
    other = [swap_pair(block, tp_size) for block in mine]
    rows = jnp.concatenate([part for k in range(lines) for part in (mine[k], other[k])], axis=0)
    blk = 2 * seq_here
    longest = seq_here * tp_size // 4
    halo = -(-longest // blk)
    ahead = halo * blk
    early_text = lax.optimization_barrier((text_rows, rows))[0]
    pieces = []
    for back in range(halo, -1, -1):
        steps = [(i, i + 2 * back) for i in range(tp_size - 2 * back)]
        ours = lax.ppermute(early_text, "tp", steps) if back else early_text
        theirs = swap_pair(ours, tp_size)
        pieces += [jnp.where(side == 0, ours, theirs), jnp.where(side == 0, theirs, ours)]
    text_normed = rms_norm(jnp.concatenate(pieces).astype(jnp.float32), dec_gain).astype(jnp.bfloat16)
    qkv_weights = gather_lines(w_qkv.T, tp_size, rows)
    out_weights = gather_lines(w_out, tp_size, qkv_weights[1])
    normed_in = layer_norm(rows.astype(jnp.float32), vis_gain).astype(jnp.bfloat16)
    hidden = jax.nn.gelu(
        jnp.dot(normed_in, w_fc1, preferred_element_type=jnp.float32), approximate=False
    ).astype(jnp.bfloat16)
    part = jnp.dot(hidden, w_fc2, preferred_element_type=jnp.float32).astype(jnp.bfloat16)
    part = part.reshape(lines, 2, local_rows, width)
    mlp_sum = jnp.zeros((local_rows, width), jnp.float32)
    for k in range(lines):
        pair = part[k, 0].astype(jnp.float32) + swap_pair(part[k, 1], tp_size).astype(jnp.float32)
        if k:
            pair = turned(pair.astype(jnp.bfloat16), tp_size, lines - k).astype(jnp.float32)
        mlp_sum = mlp_sum + pair
    normed_out = layer_norm(wide_in + mlp_sum, merge_gain).astype(jnp.bfloat16)
    quads = local_rows // 4
    blocks = normed_out.reshape(quads, lines, 2, 4 * width // tp_size)
    kept = lax.dynamic_index_in_dim(blocks, side, 2, keepdims=False)
    given = swap_pair(lax.dynamic_index_in_dim(blocks, 1 - side, 2, keepdims=False), tp_size)
    both = jnp.where(side == 0, jnp.stack([kept, given]), jnp.stack([given, kept]))
    features = jnp.zeros((lines, 2, quads, both.shape[3]), jnp.bfloat16)
    for k in range(lines):
        target = (line + k) % lines
        block = lax.dynamic_index_in_dim(both, target, 2, keepdims=False)
        if k:
            block = turned(block, tp_size, k)
        source = (line + lines - k) % lines
        features = lax.dynamic_update_index_in_dim(features, block, source, 0)
    features = features.reshape(lines * 2 * quads, both.shape[3])
    merge_term = jnp.dot(features, w_merge, preferred_element_type=jnp.float32)
    half = merge_term.shape[1] // 2
    low, high = merge_term[:, :half], merge_term[:, half:]
    sent = jnp.where(side == 0, high, low).astype(jnp.bfloat16)
    summed = jnp.where(side == 0, low, high) + swap_pair(sent, tp_size).astype(jnp.float32)
    share = summed.reshape(lines, -1, half).astype(jnp.bfloat16)
    total = lax.dynamic_index_in_dim(share, line, 0, keepdims=False).astype(jnp.float32)
    for k in range(1, lines):
        block = lax.dynamic_index_in_dim(share, (line + k) % lines, 0, keepdims=False)
        total = total + turned(block, tp_size, k).astype(jnp.float32)
    total = total.astype(jnp.bfloat16)
    gathered = jnp.zeros((lines,) + total.shape, jnp.bfloat16)
    for k in range(lines):
        block = turned(total, tp_size, k) if k else total
        gathered = lax.dynamic_update_index_in_dim(gathered, block, (line + lines - k) % lines, 0)
    gathered = gathered.reshape(-1, half)
    far = swap_pair(gathered, tp_size)
    merged = jnp.where(
        side == 0,
        jnp.concatenate([gathered, far], axis=1),
        jnp.concatenate([far, gathered], axis=1),
    )
    positions = lax.axis_index("tp") * seq_here + jnp.arange(seq_here, dtype=jnp.int32)
    matches = slot_row[None, :] == positions[:, None]
    placed = jnp.dot(
        matches.astype(jnp.bfloat16), merged, preferred_element_type=jnp.float32
    ).astype(jnp.bfloat16)
    embedded = jnp.where(jnp.any(matches, axis=1)[:, None], placed, text_rows)

    count = merged.shape[0]
    columns = qkv_weights[0].shape[0]
    depth = out_weights[0].shape[0]
    size, size_out = quarter_size(columns), quarter_size(depth)
    place = lax.axis_index("req") % 4
    starts = jnp.stack(
        [quarter_start(columns, place ^ i) for i in (0, 1, 2, 3)]
        + [quarter_start(depth, place ^ i) for i in (0, 1, 2, 3)]
        + [line * blk - ahead]
    ).astype(jnp.int32)
    smem = pl.BlockSpec(memory_space=pltpu.SMEM)

    def fixed(shape):
        return pl.BlockSpec(shape, lambda k: (0,) * len(shape))

    def moving(size):
        return pl.BlockSpec((2, 1, size, width), lambda k: (0, jnp.maximum(k - 1, 0), 0, 0))

    window = ahead + blk
    text_part = pl.pallas_call(
        text_kernel,
        grid=(lines,),
        in_specs=[smem, fixed((window, width)), fixed((columns, width)), moving(size), moving(size)],
        out_specs=pl.BlockSpec((1, columns, window), lambda k: (k, 0, 0)),
        out_shape=jax.ShapeDtypeStruct((lines, columns, window), jnp.bfloat16),
        scratch_shapes=[pltpu.VMEM((columns, width), jnp.bfloat16)],
        compiler_params=pltpu.CompilerParams(vmem_limit_bytes=40 << 20),
        cost_estimate=pl.CostEstimate(
            flops=2 * lines * columns * window * width,
            bytes_accessed=2 * lines * columns * (window + width),
            transcendentals=0,
        ),
        name="text_qkv",
    )(starts, text_normed, *qkv_weights)

    doc_window = lax.dynamic_slice_in_dim(
        jnp.concatenate([jnp.full((ahead,), -1, jnp.int32), doc_row]), line * blk, window, 0
    )
    out_part = pl.pallas_call(
        functools.partial(late_kernel, blk, longest),
        grid=(lines,),
        in_specs=[
            smem,
            fixed((count, width)),
            fixed((1, width)),
            fixed((count, 1)),
            fixed((window, 1)),
            fixed((1, blk)),
            pl.BlockSpec((1, columns, window), lambda k: (k, 0, 0)),
            fixed((columns, width)), moving(size), moving(size),
            fixed((depth, width)), moving(size_out), moving(size_out),
        ],
        out_specs=fixed((blk, width)),
        out_shape=jax.ShapeDtypeStruct((blk, width), jnp.bfloat16),
        scratch_shapes=[
            pltpu.VMEM((columns, width), jnp.bfloat16),
            pltpu.VMEM((depth, width), jnp.bfloat16),
            pltpu.VMEM((count, width), jnp.bfloat16),
            pltpu.VMEM((count, window), jnp.bfloat16),
            pltpu.VMEM((8, window), jnp.float32),
            pltpu.VMEM((blk // 128, longest + 128, 128), jnp.float32),
            pltpu.VMEM((blk, width), jnp.float32),
        ],
        compiler_params=pltpu.CompilerParams(vmem_limit_bytes=48 << 20),
        cost_estimate=pl.CostEstimate(
            flops=2 * lines * columns * (count + 2 * blk) * width,
            bytes_accessed=2 * lines * columns * (window + width),
            transcendentals=lines * columns // (3 * HD) * blk * (longest + 128),
        ),
        name="late_attention",
    )(
        starts, merged, dec_gain[None], slot_row[:, None], doc_window[:, None],
        doc_window[None, ahead:], text_part, *qkv_weights, *out_weights,
    )
    halves = out_part.reshape(2, seq_here, width)
    kept = lax.dynamic_index_in_dim(halves, side, 0, keepdims=False)
    given = swap_pair(lax.dynamic_index_in_dim(halves, 1 - side, 0, keepdims=False), tp_size)
    out_sum = kept.astype(jnp.float32) + given.astype(jnp.float32)
    decoded = (embedded.astype(jnp.float32) + out_sum).astype(jnp.bfloat16)
    return decoded[None]


def solution(mesh):
    placed = (
        P("req", "tp", None),
        P(),
        P(None, "tp"),
        P("tp", None),
        P(),
        P("tp", None),
        P("req", None),
        P("req", "tp", None),
        P("req", None),
        P(),
        P(None, "tp"),
        P("tp", None),
    )
    return jax.shard_map(
        shards, mesh=mesh, in_specs=placed, out_specs=P("req", "tp", None), check_vma=False
    )
```

```python
import functools
import math

import jax
import jax.numpy as jnp
from jax import lax
from jax.experimental import pallas as pl
from jax.experimental.pallas import tpu as pltpu
from jax.sharding import PartitionSpec as P

HD = 104
IMG_ROWS = 64


EPSILON = 1e-06


def layer_norm(values, gains):
    average = jnp.mean(values, axis=-1, keepdims=True)
    centred = values - average
    variance = jnp.mean(centred * centred, axis=-1, keepdims=True)
    return centred * lax.rsqrt(variance + EPSILON) * gains


def rms_norm(values, gains):
    return values * lax.rsqrt(jnp.mean(values * values, axis=-1, keepdims=True) + EPSILON) * gains


def pair_steps(tp_size):
    return [(i, i ^ 1) for i in range(tp_size)]


def turn_steps(tp_size, turn):
    lines = tp_size // 2
    return [(a * 2 + b, ((a + turn) % lines) * 2 + b) for a in range(lines) for b in range(2)]


def swap_pair(values, tp_size):
    return lax.ppermute(values, "tp", pair_steps(tp_size))


def turned(values, tp_size, turn):
    return lax.ppermute(values, "tp", turn_steps(tp_size, turn))


NT = (((1,), (1,)), ((), ()))
TN = (((0,), (0,)), ((), ()))


def put_quarters(whole, ours, theirs, starts, offset):
    size = ours.shape[2]
    for index in range(4):
        quarter = ours[index // 2, 0] if index % 2 == 0 else theirs[index // 2, 0]
        start = pl.multiple_of(starts[offset + index], 16)
        whole[pl.ds(start, size), :] = quarter


def put_line(whole, own, sides, middle, starts, offset, line):
    last = pl.num_programs(0) - 1

    @pl.when(line == 0)
    def _():
        whole[...] = own[...]

    @pl.when((line > 0) & (line < last))
    def _():
        put_quarters(whole, *sides, starts, offset)

    @pl.when(line == last)
    def _():
        put_quarters(whole, *middle, starts, offset)


def text_kernel(starts, gain, own, ours, theirs, *refs):
    pieces, (rows, out, whole) = refs[:-3], refs[-3:]
    step = pl.program_id(0)

    @pl.when(step == 0)
    def _():
        count = pieces[0].shape[0]
        first_side = starts[9] == 0
        for index in range(0, len(pieces), 2):
            mine, other = pieces[index][...], pieces[index + 1][...]
            both = (jnp.where(first_side, mine, other), jnp.where(first_side, other, mine))
            for half, part in enumerate(both):
                normed = rms_norm(part.astype(jnp.float32), gain[...])
                rows[pl.ds((index + half) * count, count), :] = normed.astype(jnp.bfloat16)
        whole[...] = own[...]

    @pl.when(step > 0)
    def _():
        put_quarters(whole, ours, theirs, starts, 0)

    out[0] = lax.dot_general(
        whole[...], rows[...], NT, preferred_element_type=jnp.float32
    ).astype(jnp.bfloat16)


def text_last_kernel(starts, rows, ours, theirs, before, out, whole):
    put_quarters(whole, ours, theirs, starts, 0)
    out[0] = lax.dot_general(
        whole[...], rows[...], NT, preferred_element_type=jnp.float32
    ).astype(jnp.bfloat16)


def mask_kernel(blk, longest, starts, slots, key_docs, query_docs, spread, hits, bias):
    ahead = spread.shape[1] - blk
    position = starts[8] + lax.broadcasted_iota(jnp.int32, spread.shape, 1)
    match = jnp.where(slots[...] == position, 1.0, 0.0)
    spread[...] = match.astype(jnp.bfloat16)
    hits[...] = jnp.broadcast_to(jnp.max(match, axis=0, keepdims=True), hits.shape)
    reach = longest + 128
    for block in range(blk // 128):
        first = ahead - longest + block * 128
        key_place = first + lax.broadcasted_iota(jnp.int32, (reach, 128), 0)
        query_place = ahead + block * 128 + lax.broadcasted_iota(jnp.int32, (reach, 128), 1)
        allowed = (key_place <= query_place) & (
            key_docs[pl.ds(first, reach), :] == query_docs[:, pl.ds(block * 128, 128)]
        )
        bias[block] = jnp.where(allowed, 0.0, -1e30)


def image_rows_kernel(starts, ours, theirs, gain, merged, normed):
    first_side = starts[9] == 0
    mine, other = ours[...], theirs[...]
    merged[...] = jnp.concatenate(
        [jnp.where(first_side, mine, other), jnp.where(first_side, other, mine)], axis=1
    )
    normed[...] = rms_norm(merged[...].astype(jnp.float32), gain[...]).astype(jnp.bfloat16)


def late_kernel(
    blk, longest,
    starts, image_rows, spread, hits, bias, own, ours, theirs, ours_middle, theirs_middle, text,
    kept, given, whole, blended,
):
    step = pl.program_id(0)
    put_line(whole, own, (ours, theirs), (ours_middle, theirs_middle), starts, 0, step)
    depth = blended.shape[0] // pl.num_programs(0)
    line_rows = pl.ds(pl.multiple_of(step * depth, 16), depth)
    ahead = spread.shape[1] - blk
    reach = longest + 128
    factor = math.log2(math.e) / math.sqrt(HD)
    hit = hits[0:1, :] > 0.5
    heads = whole.shape[0] // (3 * HD)
    if heads * HD < depth:
        blended[line_rows, :] = jnp.zeros((depth, blk), jnp.float32)
    image_part = lax.dot_general(
        whole[...], image_rows[...], NT, preferred_element_type=jnp.float32
    ).astype(jnp.bfloat16)
    placed = jnp.dot(image_part, spread[...], preferred_element_type=jnp.float32)
    for head in range(heads):
        base = head * 3 * HD

        def picked(part, start):
            rows = pl.ds(base + part * HD, HD)
            image = placed[base + part * HD : base + (part + 1) * HD, start:]
            return jnp.where(hit[:, start:], image, text[0, rows, start:].astype(jnp.float32))

        queries = (picked(0, ahead) * factor).astype(jnp.bfloat16)
        keys = picked(1, 0).T.astype(jnp.bfloat16)
        values = picked(2, 0).astype(jnp.bfloat16)
        for block in range(blk // 128):
            first = ahead - longest + block * 128
            columns = pl.ds(block * 128, 128)
            scores = jnp.dot(
                keys[first : first + reach],
                queries[:, block * 128 : block * 128 + 128],
                preferred_element_type=jnp.float32,
            ) + bias[block]
            raised = jnp.exp2(scores - jnp.max(scores, axis=0, keepdims=True))
            mixed = jnp.dot(
                values[:, first : first + reach],
                raised.astype(jnp.bfloat16),
                preferred_element_type=jnp.float32,
            )
            share = 1.0 / jnp.sum(raised, axis=0, keepdims=True)
            blended[pl.ds(pl.multiple_of(step * depth + head * HD, 8), HD), columns] = mixed * share

    @pl.when(step == pl.num_programs(0) - 1)
    def _():
        attended = blended[...].T.astype(jnp.bfloat16)
        half = blk // 2
        low, high = attended[:half], attended[half:]
        first_side = starts[9] == 0
        kept[...] = jnp.where(first_side, low, high)
        given[...] = jnp.where(first_side, high, low)


def project_kernel(starts, rows, own, ours, theirs, out, whole):
    depth = own.shape[0]
    whole[:depth] = own[...]
    size = ours.shape[2]
    for line in range(ours.shape[1]):
        for index in range(4):
            quarter = (ours if index % 2 == 0 else theirs)[index // 2, line]
            start = pl.multiple_of((line + 1) * depth + starts[4 + index], 16)
            whole[pl.ds(start, size), :] = quarter
    total = jnp.dot(rows[...], whole[...], preferred_element_type=jnp.float32)
    out[...] = total.astype(jnp.bfloat16)


def out_kernel(starts, text, slots, merged, kept, got, out):
    count = text.shape[0]
    position = starts[10] + lax.broadcasted_iota(jnp.int32, (count, merged.shape[0]), 0)
    match = jnp.where(slots[...] == position, 1.0, 0.0)
    placed = jnp.dot(match.astype(jnp.bfloat16), merged[...], preferred_element_type=jnp.float32)
    hit = jnp.max(match, axis=1, keepdims=True) > 0.5
    embedded = jnp.where(hit, placed, text[...].astype(jnp.float32))
    total = kept[...].astype(jnp.float32) + got[...].astype(jnp.float32)
    out[...] = (embedded + total).astype(jnp.bfloat16)


SMEM = pl.BlockSpec(memory_space=pltpu.SMEM)


def kernel_call(body, name, results, *operands, scratch=(), grid=(), specs={}, out_specs=None, aliases={}):
    return pl.pallas_call(
        body,
        grid=grid,
        in_specs=[SMEM]
        + [
            specs.get(place, whole_block(value.shape))
            for place, value in enumerate(operands)
            if place
        ],
        out_specs=out_specs or [whole_block(shape) for shape, _ in results],
        out_shape=[jax.ShapeDtypeStruct(shape, dtype) for shape, dtype in results],
        scratch_shapes=list(scratch),
        input_output_aliases=aliases,
        compiler_params=pltpu.CompilerParams(vmem_limit_bytes=56 << 20),
        cost_estimate=pl.CostEstimate(flops=1, bytes_accessed=1, transcendentals=0),
        name=name,
    )(*operands)


def quarters_spec(values, line_of):
    shape = (2, 1) + values.shape[2:]
    return pl.BlockSpec(shape, lambda k: (0, line_of(k), 0, 0))


def project(starts, rows, own, ours, theirs):
    lines = ours.shape[1] + 1
    return kernel_call(
        project_kernel, "project", [((rows.shape[0], own.shape[1]), jnp.bfloat16)],
        starts, rows, own, ours, theirs,
        scratch=[pltpu.VMEM((lines * own.shape[0], own.shape[1]), jnp.bfloat16)],
    )


def mlp_kernel(mine, other, gain, w_in, w_back, out_mine, out_other, rows, total):
    step = pl.program_id(0)
    count = mine.shape[0]

    @pl.when(step == 0)
    def _():
        for place, part in ((0, mine), (count, other)):
            normed = layer_norm(part[...].astype(jnp.float32), gain[...])
            rows[pl.ds(place, count), :] = normed.astype(jnp.bfloat16)
        total[...] = jnp.zeros_like(total)

    wide = jnp.dot(rows[...], w_in[...], preferred_element_type=jnp.float32)
    hidden = 0.5 * wide * (1.0 + lax.erf(wide * math.sqrt(0.5)))
    total[...] += jnp.dot(
        hidden.astype(jnp.bfloat16), w_back[...], preferred_element_type=jnp.float32
    )

    @pl.when(step == pl.num_programs(0) - 1)
    def _():
        out_mine[...] = total[:count].astype(jnp.bfloat16)
        out_other[...] = total[count:].astype(jnp.bfloat16)


def whole_block(shape):
    return pl.BlockSpec(shape, lambda *_: (0,) * len(shape))


def mlp(mine, other, gain, w_in, w_back):
    count, width = mine.shape
    units = w_in.shape[1]
    step = 256
    return pl.pallas_call(
        mlp_kernel,
        grid=(units // step,),
        in_specs=[
            whole_block((count, width)),
            whole_block((count, width)),
            whole_block((1, width)),
            pl.BlockSpec((width, step), lambda i: (0, i)),
            pl.BlockSpec((step, width), lambda i: (i, 0)),
        ],
        out_specs=[whole_block((count, width))] * 2,
        out_shape=[jax.ShapeDtypeStruct((count, width), jnp.bfloat16)] * 2,
        scratch_shapes=[
            pltpu.VMEM((2 * count, width), jnp.bfloat16),
            pltpu.VMEM((2 * count, width), jnp.float32),
        ],
        compiler_params=pltpu.CompilerParams(vmem_limit_bytes=16 << 20),
        cost_estimate=pl.CostEstimate(flops=1, bytes_accessed=1, transcendentals=0),
        name="mlp_rows",
    )(mine, other, gain[None], w_in, w_back)


def spread_kernel(lines, place, rows, *refs):
    parts, (gain, kept, given) = refs[:-3], refs[-3:]
    wide = rows[...].astype(jnp.float32)
    for part in parts:
        wide = wide + part[...].astype(jnp.float32)
    normed = layer_norm(wide, gain[...]).astype(jnp.bfloat16)
    size = kept.shape[2]
    quads = kept.shape[1]
    to = lax.broadcasted_iota(jnp.int32, (4 * quads, 4 * quads), 0)
    by = lax.broadcasted_iota(jnp.int32, (4 * quads, 4 * quads), 1)
    moves = jnp.where(by == to % quads * 4 + to // quads, 1.0, 0.0).astype(jnp.bfloat16)
    sorted_rows = jnp.dot(moves, normed, preferred_element_type=jnp.float32).astype(jnp.bfloat16)
    first_side = place[0] == 0
    for target in range(lines):
        row, base = target // (lines // 4), target % (lines // 4) * 2 * size
        picked = sorted_rows[row * quads : (row + 1) * quads]
        low, high = picked[:, base : base + size], picked[:, base + size : base + 2 * size]
        turn = lax.rem(target + lines - place[1], lines)
        kept[turn] = jnp.where(first_side, low, high)
        given[turn] = jnp.where(first_side, high, low)


def spread_rows(place, rows, parts, gain, lines):
    count, width = rows.shape
    shape = (lines, count // 4, 2 * width // lines)
    return pl.pallas_call(
        functools.partial(spread_kernel, lines),
        in_specs=[pl.BlockSpec(memory_space=pltpu.SMEM)]
        + [whole_block((count, width))] * (1 + len(parts))
        + [whole_block((1, width))],
        out_specs=[whole_block(shape)] * 2,
        out_shape=[jax.ShapeDtypeStruct(shape, jnp.bfloat16)] * 2,
        compiler_params=pltpu.CompilerParams(vmem_limit_bytes=56 << 20),
        cost_estimate=pl.CostEstimate(flops=1, bytes_accessed=1, transcendentals=0),
        name="spread_rows",
    )(place, rows, *parts, gain[None])


def merge_kernel(place, *refs):
    blocks, (weights, kept, given, rows) = refs[:-4], refs[-4:]
    lines = len(blocks)
    quads = blocks[0].shape[0] // 2
    for index, block in enumerate(blocks):
        base = lax.rem(place[1] + lines - index, lines) * 2
        for half in (0, 1):
            start = (base + (place[0] if half == 0 else 1 - place[0])) * quads
            rows[pl.ds(pl.multiple_of(start, 16), quads), :] = block[half * quads : half * quads + quads]
    wide = jnp.dot(rows[...], weights[...], preferred_element_type=jnp.float32)
    half = kept.shape[1]
    low, high = wide[:, :half], wide[:, half:]
    first_side = place[0] == 0
    kept[...] = jnp.where(first_side, low, high)
    given[...] = jnp.where(first_side, high, low).astype(jnp.bfloat16)


def split_kernel(needed, place, kept, got, *outs):
    for index, out in enumerate(outs):
        for image in range(needed):
            rows = pl.ds(pl.multiple_of(place[2 + index * needed + image] * IMG_ROWS, 16), IMG_ROWS)
            both = kept[rows, :] + got[rows, :].astype(jnp.float32)
            out[image * IMG_ROWS : (image + 1) * IMG_ROWS] = both.astype(jnp.bfloat16)


def merge(place, blocks, weights):
    count, size = blocks[0].shape
    rows, half = count * len(blocks), weights.shape[1] // 2
    return pl.pallas_call(
        merge_kernel,
        in_specs=[pl.BlockSpec(memory_space=pltpu.SMEM)]
        + [whole_block((count, size))] * len(blocks)
        + [whole_block(weights.shape)],
        out_specs=[whole_block((rows, half))] * 2,
        out_shape=[
            jax.ShapeDtypeStruct((rows, half), jnp.float32),
            jax.ShapeDtypeStruct((rows, half), jnp.bfloat16),
        ],
        scratch_shapes=[pltpu.VMEM((rows, size), jnp.bfloat16)],
        compiler_params=pltpu.CompilerParams(vmem_limit_bytes=56 << 20),
        cost_estimate=pl.CostEstimate(flops=1, bytes_accessed=1, transcendentals=0),
        name="merge_rows",
    )(place, *blocks, weights)


def after(values, first):
    return lax.optimization_barrier((values, first))[0]


class Queue:
    def __init__(self):
        self.last = []

    def held(self, value):
        return after(value, self.last) if self.last else value

    def passed(self, value):
        self.last = [value]
        return value

    def wait(self, value):
        self.last = self.last + [value]
        return value


def quarter_size(rows):
    return -(-rows // 64) * 16


def quarter_start(rows, index):
    return jnp.minimum(index * quarter_size(rows), rows - quarter_size(rows))


def padded(weights):
    return jnp.pad(weights, ((0, -weights.shape[0] % 16), (0, 0)))


def own_quarter(weights):
    place = lax.axis_index("req") % 4
    size = quarter_size(weights.shape[0])
    return lax.dynamic_slice_in_dim(weights, quarter_start(weights.shape[0], place), size, 0)


def other_copy(values, flip):
    return lax.ppermute(values, "req", [(i, i ^ flip) for i in range(lax.axis_size("req"))])


def line_neighbours(values, tp_size):
    lines = tp_size // 2
    if lines != 4:
        return [turned(values, tp_size, k) for k in range(1, lines)]
    up = lax.ppermute(values, "tp", [(i, i + 2) for i in range(tp_size - 2)])
    down = lax.ppermute(values, "tp", [(i + 2, i) for i in range(tp_size - 2)])
    return [up, turned(values, tp_size, 2), down]


def line_ends(parts, tp_size, queue):
    if tp_size // 2 != 4:
        return parts
    line = lax.axis_index("tp") // 2
    ends = lax.ppermute(queue.held(parts[1]), "tp", [(2, 0), (3, 1), (4, 6), (5, 7)])
    return [jnp.where(line == 0, ends, parts[0]), parts[1], jnp.where(line == 3, ends, parts[2])]


def shards(
    patches, vis_gain, w_fc1, w_fc2, merge_gain, w_merge, slots, text, docs, dec_gain, w_qkv, w_out
):
    patch_rows = patches[0]
    slot_row = slots[0]
    text_rows = text[0]
    doc_row = docs[0]
    width = patch_rows.shape[1]
    seq_here = text_rows.shape[0]
    tp_size = lax.axis_size("tp")
    lines = tp_size // 2
    line = lax.axis_index("tp") // 2
    side = lax.axis_index("tp") % 2
    place_here = jnp.stack([side, line]).astype(jnp.int32)

    blk = 2 * seq_here
    longest = seq_here * tp_size // 4
    halo = -(-longest // blk)
    ahead = halo * blk
    window = ahead + blk
    qkv_own = padded(w_qkv.T)
    out_own = padded(w_out)
    columns, depth = qkv_own.shape[0], out_own.shape[0]
    place = lax.axis_index("req") % 4
    starts = jnp.stack(
        [quarter_start(columns, place ^ i) for i in (0, 1, 2, 3)]
        + [quarter_start(depth, place ^ i) for i in (0, 1, 2, 3)]
        + [line * blk - ahead, side, (2 * line + side) * seq_here]
    ).astype(jnp.int32)
    bf16 = jnp.bfloat16

    images = slot_row.shape[0] // IMG_ROWS
    span = seq_here * tp_size // images
    tables = []
    for target in range(lines):
        held = []
        for place_of in range(images):
            low = place_of * span if place_of < images - 1 else images * span - IMG_ROWS
            inside = low < (target + 1) * blk and (place_of + 1) * span > target * blk - ahead
            held.append((not inside, (place_of - images // 2) % images))
        tables.append(sorted(held))
    needed = max(sum(not outside for outside, _ in held) for held in tables)
    table = jnp.array([[image for _, image in held[:needed]] for held in tables], jnp.int32)
    turned_table = table[(line + jnp.arange(lines)) % lines]
    place_here = jnp.concatenate([place_here, turned_table.reshape(-1)])
    by_image = slot_row.reshape(images, IMG_ROWS)
    slot_row = jnp.concatenate(
        [lax.dynamic_index_in_dim(by_image, turned_table[0, i], 0, False) for i in range(needed)]
    )
    count = needed * IMG_ROWS
    doc_window = lax.dynamic_slice_in_dim(
        jnp.concatenate([jnp.full((ahead,), -1, jnp.int32), doc_row]), line * blk, window, 0
    )

    queue = Queue()
    rounds = [k for k in range(1, lines) if k != lines // 2]
    middle = lines // 2
    other, sums, part = {}, {}, {}

    def run_mlp(k, mine):
        own, given = mlp(queue.held(mine), other[k], vis_gain, w_fc1, w_fc2)
        queue.passed((own, given))
        part[k] = own
        return swap_pair(given, tp_size)

    def add_pair(k, got):
        pair = (queue.held(part[k]).astype(jnp.float32) + got.astype(jnp.float32)).astype(bf16)
        queue.passed(pair)
        return turned(pair, tp_size, lines - k)

    swapping = swap_pair(patch_rows, tp_size)
    moving = {k: turned(patch_rows, tp_size, k) for k in rounds + [middle]}
    other[0] = queue.wait(swapping)
    text_back = []
    for steps_back in range(1, halo + 1):
        steps = [(i, i + 2 * steps_back) for i in range(tp_size - 2 * steps_back)]
        text_back.append(lax.ppermute(queue.held(text_rows), "tp", steps))
    text_other = swap_pair(queue.held(text_rows), tp_size)
    back = {0: run_mlp(0, patch_rows)}
    mine, swapping = {}, {}
    for k in rounds + [middle]:
        mine[k] = queue.wait(moving[k])
        swapping[k] = swap_pair(queue.held(mine[k]), tp_size)
    qkv_quarter, out_quarter = own_quarter(qkv_own), own_quarter(out_own)
    qkv_moving = {}

    def move_weights(k):
        qkv_moving[k] = turned(queue.held(qkv_quarter), tp_size, k)

    move_weights(rounds[0])
    for index, k in enumerate(rounds):
        other[k] = queue.wait(swapping[k])
        if index == 1:
            text_other = queue.wait(text_other)
            text_back = queue.wait(text_back)
        back[k] = run_mlp(k, mine[k])
    for index, k in enumerate(rounds):
        queue.wait(qkv_moving[k])
        if index + 1 < len(rounds):
            move_weights(rounds[index + 1])
        if index == 0:
            other[middle] = queue.wait(swapping[middle])
            back[middle] = run_mlp(middle, mine[middle])
            for j in rounds:
                sums[j] = add_pair(j, queue.wait(back[j]))
    for k in rounds:
        queue.wait(sums[k])
    sides = queue.passed(jnp.stack([queue.held(qkv_moving[k]) for k in rounds]))
    sides_far = other_copy(sides, 2)
    sums[middle] = add_pair(middle, queue.wait(back[middle]))
    pieces = []
    for rows in text_back[::-1]:
        pieces += [rows, swap_pair(queue.held(rows), tp_size)]
    spread, hits, bias = queue.passed(kernel_call(
        functools.partial(mask_kernel, blk, longest), "masks",
        [
            ((count, window), bf16),
            ((8, window), jnp.float32),
            ((blk // 128, longest + 128, 128), jnp.float32),
        ],
        starts, queue.held(slot_row[:, None]), doc_window[:, None], doc_window[None, ahead:],
    ))
    sums[0] = part[0]
    sums = [queue.wait(back[0])] + [queue.wait(sums[k]) for k in range(lines)]
    move_weights(middle)
    kept, given = queue.passed(
        spread_rows(place_here, queue.held(patch_rows), sums, merge_gain, lines)
    )
    pieces = queue.wait(pieces) + [text_rows, text_other]
    got = swap_pair(queue.held(given), tp_size)
    sides_ours = queue.passed(jnp.stack([queue.held(sides), queue.wait(sides_far)]))
    sides_theirs = other_copy(sides_ours, 1)
    got = queue.wait(got)
    blocks = queue.passed([jnp.concatenate([queue.held(kept[k]), got[k]]) for k in range(lines)])
    blocks = [blocks[0]] + [turned(blocks[k], tp_size, k) for k in range(1, lines)]
    sides_theirs = queue.wait(sides_theirs)

    def after_own(k):
        return jnp.clip(k - 1, 0, lines - 3)

    text_normed, text_parts = queue.passed(kernel_call(
        text_kernel, "text_qkv", [((window, width), bf16), ((lines, columns, window), bf16)],
        starts, queue.held(dec_gain[None]), qkv_own, sides_ours, sides_theirs, *pieces,
        grid=(lines - 1,),
        specs={place: quarters_spec(sides_ours, after_own) for place in (3, 4)},
        out_specs=[
            whole_block((window, width)),
            pl.BlockSpec((1, columns, window), lambda k: (k, 0, 0)),
        ],
        scratch=[pltpu.VMEM((columns, width), bf16)],
    ))
    queue.wait(blocks)
    kept, given = queue.passed(merge(place_here, [queue.held(blocks[0])] + blocks[1:], w_merge))
    half = kept.shape[1]
    got = swap_pair(given, tp_size)
    middle_near = queue.wait(qkv_moving[middle])
    middle_far = other_copy(queue.held(middle_near), 2)
    share = queue.passed(kernel_call(
        functools.partial(split_kernel, needed), "image_shares", [((count, half), bf16)] * lines,
        place_here, queue.held(kept), queue.wait(got),
    ))
    moving = [turned(share[k], tp_size, k) for k in range(1, lines)]
    out_moving = [turned(queue.held(out_quarter), tp_size, k) for k in rounds + [middle]]
    middle_ours = queue.passed(jnp.stack([queue.held(middle_near), queue.wait(middle_far)])[:, None])
    middle_theirs = other_copy(middle_ours, 1)
    total = queue.held(share[0]).astype(jnp.float32)
    for block in queue.wait(moving):
        total = total + block.astype(jnp.float32)
    total = queue.passed(total.astype(bf16))
    far = swap_pair(total, tp_size)
    (text_parts,) = queue.passed(kernel_call(
        text_last_kernel, "text_last", [((lines, columns, window), bf16)],
        starts, queue.held(text_normed), middle_ours, queue.wait(middle_theirs), text_parts,
        grid=(1,),
        specs={4: pl.BlockSpec(memory_space=pl.ANY)},
        out_specs=[pl.BlockSpec((1, columns, window), lambda k: (lines - 1, 0, 0))],
        scratch=[pltpu.VMEM((columns, width), bf16)],
        aliases={4: 0},
    ))
    merged, image_rows = queue.passed(kernel_call(
        image_rows_kernel, "image_rows", [((count, width), bf16)] * 2,
        starts, queue.held(total), queue.wait(far), dec_gain[None],
    ))
    out_near = queue.passed(jnp.stack(queue.wait([queue.held(part) for part in out_moving])))
    out_far = other_copy(out_near, 2)
    kept, given = queue.passed(kernel_call(
        functools.partial(late_kernel, blk, longest), "late_attention",
        [((seq_here, lines * depth), bf16)] * 2,
        starts, queue.held(image_rows), spread, hits, bias,
        qkv_own, sides_ours, sides_theirs, middle_ours, middle_theirs, text_parts,
        grid=(lines,),
        specs={
            6: quarters_spec(sides_ours, after_own),
            7: quarters_spec(sides_ours, after_own),
            10: pl.BlockSpec((1, columns, window), lambda k: (k, 0, 0)),
        },
        scratch=[pltpu.VMEM((columns, width), bf16), pltpu.VMEM((lines * depth, blk), jnp.float32)],
    ))
    out_ours = queue.passed(jnp.stack([queue.held(out_near), queue.wait(out_far)]))
    out_theirs = other_copy(out_ours, 1)
    (given,) = queue.passed(project(starts, queue.held(given), out_own, out_ours, queue.wait(out_theirs)))
    got = swap_pair(given, tp_size)
    (kept,) = queue.passed(project(starts, queue.held(kept), out_own, out_ours, out_theirs))
    (decoded,) = kernel_call(
        out_kernel, "out_rows", [((seq_here, width), bf16)],
        starts, queue.held(text_rows), slot_row[None], merged, kept, queue.wait(got),
    )
    return decoded[None]


def solution(mesh):
    placed = (
        P("req", "tp", None),
        P(),
        P(None, "tp"),
        P("tp", None),
        P(),
        P("tp", None),
        P("req", None),
        P("req", "tp", None),
        P("req", None),
        P(),
        P(None, "tp"),
        P("tp", None),
    )
    return jax.shard_map(
        shards, mesh=mesh, in_specs=placed, out_specs=P("req", "tp", None), check_vma=False
    )
```

```python
import functools
import math

import jax
import jax.numpy as jnp
from jax import lax
from jax.experimental import pallas as pl
from jax.experimental.pallas import tpu as pltpu
from jax.sharding import PartitionSpec as P

HD = 104
IMG_ROWS = 64
TABLE = 12


EPSILON = 1e-06


def layer_norm(values, gains):
    average = jnp.mean(values, axis=-1, keepdims=True)
    centred = values - average
    variance = jnp.mean(centred * centred, axis=-1, keepdims=True)
    return centred * lax.rsqrt(variance + EPSILON) * gains


def rms_norm(values, gains):
    return values * lax.rsqrt(jnp.mean(values * values, axis=-1, keepdims=True) + EPSILON) * gains


def pair_steps(tp_size):
    return [(i, i ^ 1) for i in range(tp_size)]


def turn_steps(tp_size, turn):
    lines = tp_size // 2
    return [(a * 2 + b, ((a + turn) % lines) * 2 + b) for a in range(lines) for b in range(2)]


def swap_pair(values, tp_size):
    return lax.ppermute(values, "tp", pair_steps(tp_size))


def turned(values, tp_size, turn):
    return lax.ppermute(values, "tp", turn_steps(tp_size, turn))


NT = (((1,), (1,)), ((), ()))
TN = (((0,), (0,)), ((), ()))


def put_quarters(whole, ours, theirs, starts, offset):
    size = ours.shape[2]
    for index in range(4):
        quarter = ours[index // 2, 0] if index % 2 == 0 else theirs[index // 2, 0]
        start = pl.multiple_of(starts[offset + index], 16)
        whole[pl.ds(start, size), :] = quarter


def text_kernel(starts, gain, own, *refs):
    pieces, (rows, out) = refs[:-2], refs[-2:]
    count = pieces[0].shape[0]
    first_side = starts[9] == 0
    for index in range(0, len(pieces), 2):
        mine, other = pieces[index][...], pieces[index + 1][...]
        both = (jnp.where(first_side, mine, other), jnp.where(first_side, other, mine))
        for half, part in enumerate(both):
            normed = rms_norm(part.astype(jnp.float32), gain[...].reshape(1, -1))
            rows[pl.ds((index + half) * count, count), :] = normed.astype(jnp.bfloat16)
    out[0] = lax.dot_general(
        own[...], rows[...], NT, preferred_element_type=jnp.float32
    ).astype(jnp.bfloat16)


def text_next_kernel(starts, rows, ours, theirs, before, out, whole):
    @pl.when(pl.program_id(0) == 0)
    def _():
        put_quarters(whole, ours, theirs, starts, 0)

    out[0] = lax.dot_general(
        whole[...], rows[...], NT, preferred_element_type=jnp.float32
    ).astype(jnp.bfloat16)


def mask_kernel(blk, longest, starts, slots, docs, spread, hits, bias, slots_here):
    count, window = spread.shape
    ahead = window - blk
    for index in range(count // IMG_ROWS):
        picked = slots[:, :IMG_ROWS]
        for image in range(1, slots.shape[1] // IMG_ROWS):
            rows = slots[:, image * IMG_ROWS : (image + 1) * IMG_ROWS]
            picked = jnp.where(starts[TABLE + index] == image, rows, picked)
        slots_here[:, index * IMG_ROWS : (index + 1) * IMG_ROWS] = jnp.broadcast_to(
            picked, (8, IMG_ROWS)
        )
    slot_columns = jnp.broadcast_to(slots_here[0:1, :].astype(jnp.float32), (128, count)).T
    position = starts[8] + lax.broadcasted_iota(jnp.int32, spread.shape, 1)
    match = jnp.where(slot_columns[:, 0:1] == position.astype(jnp.float32), 1.0, 0.0)
    spread[...] = match.astype(jnp.bfloat16)
    hits[...] = jnp.broadcast_to(jnp.max(match, axis=0, keepdims=True), hits.shape)
    line = starts[11]
    parts = []
    for back in range(ahead // blk, -1, -1):
        start = pl.multiple_of(jnp.maximum(line - back, 0) * blk, 128)
        part = docs[:, pl.ds(start, blk)].astype(jnp.float32)
        parts.append(jnp.where(line >= back, part, -1.0))
    doc_row = jnp.concatenate(parts, axis=1)
    doc_columns = jnp.broadcast_to(doc_row, (128, window)).T
    reach = longest + 128
    for block in range(blk // 128):
        first = ahead - longest + block * 128
        key_place = first + lax.broadcasted_iota(jnp.int32, (reach, 128), 0)
        query_place = ahead + block * 128 + lax.broadcasted_iota(jnp.int32, (reach, 128), 1)
        query_docs = doc_row[:, ahead + block * 128 : ahead + block * 128 + 128]
        allowed = (key_place <= query_place) & (doc_columns[first : first + reach] == query_docs)
        bias[block] = jnp.where(allowed, 0.0, -1e30)


def image_rows_kernel(starts, ours, theirs, gain, merged, normed):
    first_side = starts[9] == 0
    mine, other = ours[...], theirs[...]
    merged[...] = jnp.concatenate(
        [jnp.where(first_side, mine, other), jnp.where(first_side, other, mine)], axis=1
    )
    normed[...] = rms_norm(merged[...].astype(jnp.float32), gain[...].reshape(1, -1)).astype(jnp.bfloat16)


def late_kernel(blk, longest, lines, depth, starts, image_rows, spread, hits, bias, *refs):
    sources, near = refs[: 2 * lines], refs[2 * lines + 2 : 4 * lines + 2]
    kept, given = refs[2 * lines : 2 * lines + 2]
    whole, blended, arrived = refs[-3:]
    texts, text_near = sources[0], near[0]
    copies = [pltpu.make_async_copy(texts.at[0], text_near.at[0], arrived.at[0])]
    copies.append(pltpu.make_async_copy(sources[1], near[1], arrived.at[1]))
    for line in range(1, lines):
        for place in (2 * line, 2 * line + 1):
            copies.append(pltpu.make_async_copy(sources[place], near[place], arrived.at[place]))
        copies.append(
            pltpu.make_async_copy(texts.at[line], text_near.at[line], arrived.at[2 * lines + line])
        )
    for copy in copies:
        copy.start()
    ahead = spread.shape[1] - blk
    reach = longest + 128
    factor = math.log2(math.e) / math.sqrt(HD)
    hit = hits[0:1, :] > 0.5
    heads = near[1].shape[0] // (3 * HD)
    if heads * HD < depth:
        blended[...] = jnp.zeros_like(blended)
    for line in range(lines):
        for copy in copies[: 2] if line == 0 else copies[3 * line - 1 : 3 * line + 2]:
            copy.wait()
        if line:
            put_quarters(whole, near[2 * line], near[2 * line + 1], starts, 0)
        weights = whole if line else near[1]
        image_part = lax.dot_general(
            image_rows[...], weights[...], NT, preferred_element_type=jnp.float32
        ).astype(jnp.bfloat16)
        placed = lax.dot_general(
            image_part, spread[...], TN, preferred_element_type=jnp.float32
        )
        for head in range(heads):
            base = head * 3 * HD

            def picked(part, start):
                rows = pl.ds(base + part * HD, HD)
                image = placed[base + part * HD : base + (part + 1) * HD, start:]
                text = text_near[line, rows, start:].astype(jnp.float32)
                return jnp.where(hit[:, start:], image, text)

            queries = (picked(0, ahead) * factor).astype(jnp.bfloat16)
            keys = picked(1, 0).T.astype(jnp.bfloat16)
            values = picked(2, 0).astype(jnp.bfloat16)
            blocks = range(blk // 128)
            firsts = [ahead - longest + block * 128 for block in blocks]
            scores = [
                jnp.dot(
                    keys[first : first + reach],
                    queries[:, block * 128 : block * 128 + 128],
                    preferred_element_type=jnp.float32,
                ) + bias[block]
                for block, first in zip(blocks, firsts)
            ]
            raised = [jnp.exp2(part - jnp.max(part, axis=0, keepdims=True)) for part in scores]
            shares = [1.0 / jnp.sum(part, axis=0, keepdims=True) for part in raised]
            mixed = [
                jnp.dot(
                    values[:, first : first + reach],
                    part.astype(jnp.bfloat16),
                    preferred_element_type=jnp.float32,
                )
                for first, part in zip(firsts, raised)
            ]
            for block in blocks:
                columns = pl.ds(block * 128, 128)
                blended[pl.ds(line * depth + head * HD, HD), columns] = mixed[block] * shares[block]
    attended = blended[...].T.astype(jnp.bfloat16)
    low, high = attended[: blk // 2], attended[blk // 2 :]
    first_side = starts[9] == 0
    kept[...] = jnp.where(first_side, low, high)
    given[...] = jnp.where(first_side, high, low)


def project_kernel(starts, rows, own, ours, theirs, out, whole):
    depth = own.shape[0]
    whole[:depth] = own[...]
    size = ours.shape[2]
    for line in range(ours.shape[1]):
        for index in range(4):
            quarter = (ours if index % 2 == 0 else theirs)[index // 2, line]
            start = pl.multiple_of((line + 1) * depth + starts[4 + index], 16)
            whole[pl.ds(start, size), :] = quarter
    total = jnp.dot(rows[...], whole[...], preferred_element_type=jnp.float32)
    out[...] = total.astype(jnp.bfloat16)


def out_kernel(starts, text, slots, merged, kept, got, out):
    count = text.shape[0]
    position = starts[10] + lax.broadcasted_iota(jnp.int32, (count, merged.shape[0]), 0)
    match = jnp.where(slots[0:1, :] == position, 1.0, 0.0)
    placed = jnp.dot(match.astype(jnp.bfloat16), merged[...], preferred_element_type=jnp.float32)
    hit = jnp.max(match, axis=1, keepdims=True) > 0.5
    embedded = jnp.where(hit, placed, text[...].astype(jnp.float32))
    total = kept[...].astype(jnp.float32) + got[...].astype(jnp.float32)
    out[...] = (embedded + total).astype(jnp.bfloat16)


SMEM = pl.BlockSpec(memory_space=pltpu.SMEM)


def kernel_call(body, name, results, *operands, scratch=(), grid=(), specs={}, out_specs=None, aliases={}):
    return pl.pallas_call(
        body,
        grid=grid,
        in_specs=[SMEM]
        + [
            specs.get(place, whole_block(value.shape))
            for place, value in enumerate(operands)
            if place
        ],
        out_specs=out_specs or [whole_block(shape) for shape, _ in results],
        out_shape=[jax.ShapeDtypeStruct(shape, dtype) for shape, dtype in results],
        scratch_shapes=list(scratch),
        input_output_aliases=aliases,
        compiler_params=pltpu.CompilerParams(vmem_limit_bytes=56 << 20),
        cost_estimate=pl.CostEstimate(flops=1, bytes_accessed=1, transcendentals=0),
        name=name,
    )(*operands)


def quarters_spec(values, line_of):
    shape = (2, 1) + values.shape[2:]
    return pl.BlockSpec(shape, lambda k: (0, line_of(k), 0, 0))


def project(starts, rows, own, ours, theirs):
    lines = ours.shape[1] + 1
    return kernel_call(
        project_kernel, "project", [((rows.shape[0], own.shape[1]), jnp.bfloat16)],
        starts, rows, own, ours, theirs,
        scratch=[pltpu.VMEM((lines * own.shape[0], own.shape[1]), jnp.bfloat16)],
    )


def mlp_kernel(mine, other, gain, w_in, w_back, out_mine, out_other, rows, total):
    step = pl.program_id(0)
    count = mine.shape[0]

    @pl.when(step == 0)
    def _():
        for place, part in ((0, mine), (count, other)):
            normed = layer_norm(part[...].astype(jnp.float32), gain[...].reshape(1, -1))
            rows[pl.ds(place, count), :] = normed.astype(jnp.bfloat16)
        total[...] = jnp.zeros_like(total)

    wide = jnp.dot(rows[...], w_in[...], preferred_element_type=jnp.float32)
    hidden = 0.5 * wide * (1.0 + lax.erf(wide * math.sqrt(0.5)))
    total[...] += jnp.dot(
        hidden.astype(jnp.bfloat16), w_back[...], preferred_element_type=jnp.float32
    )

    @pl.when(step == pl.num_programs(0) - 1)
    def _():
        out_mine[...] = total[:count].astype(jnp.bfloat16)
        out_other[...] = total[count:].astype(jnp.bfloat16)


def whole_block(shape):
    return pl.BlockSpec(shape, lambda *_: (0,) * len(shape))


def mlp(mine, other, gain, w_in, w_back):
    count, width = mine.shape
    units = w_in.shape[1]
    step = 256
    return pl.pallas_call(
        mlp_kernel,
        grid=(units // step,),
        in_specs=[
            whole_block((count, width)),
            whole_block((count, width)),
            whole_block((width,)),
            pl.BlockSpec((width, step), lambda i: (0, i)),
            pl.BlockSpec((step, width), lambda i: (i, 0)),
        ],
        out_specs=[whole_block((count, width))] * 2,
        out_shape=[jax.ShapeDtypeStruct((count, width), jnp.bfloat16)] * 2,
        scratch_shapes=[
            pltpu.VMEM((2 * count, width), jnp.bfloat16),
            pltpu.VMEM((2 * count, width), jnp.float32),
        ],
        compiler_params=pltpu.CompilerParams(vmem_limit_bytes=16 << 20),
        cost_estimate=pl.CostEstimate(flops=1, bytes_accessed=1, transcendentals=0),
        name="mlp_rows",
    )(mine, other, gain, w_in, w_back)


def spread_kernel(lines, place, rows, *refs):
    parts, (gain, kept, given) = refs[:-3], refs[-3:]
    wide = rows[...].astype(jnp.float32)
    for part in parts:
        wide = wide + part[...].astype(jnp.float32)
    normed = layer_norm(wide, gain[...].reshape(1, -1)).astype(jnp.bfloat16)
    size = kept.shape[2]
    quads = kept.shape[1]
    to = lax.broadcasted_iota(jnp.int32, (4 * quads, 4 * quads), 0)
    by = lax.broadcasted_iota(jnp.int32, (4 * quads, 4 * quads), 1)
    moves = jnp.where(by == to % quads * 4 + to // quads, 1.0, 0.0).astype(jnp.bfloat16)
    sorted_rows = jnp.dot(moves, normed, preferred_element_type=jnp.float32).astype(jnp.bfloat16)
    first_side = place[9] == 0
    for target in range(lines):
        row, base = target // (lines // 4), target % (lines // 4) * 2 * size
        picked = sorted_rows[row * quads : (row + 1) * quads]
        low, high = picked[:, base : base + size], picked[:, base + size : base + 2 * size]
        turn = lax.rem(target + lines - place[11], lines)
        kept[turn] = jnp.where(first_side, low, high)
        given[turn] = jnp.where(first_side, high, low)


def spread_rows(place, rows, parts, gain, lines):
    count, width = rows.shape
    shape = (lines, count // 4, 2 * width // lines)
    return pl.pallas_call(
        functools.partial(spread_kernel, lines),
        in_specs=[pl.BlockSpec(memory_space=pltpu.SMEM)]
        + [whole_block((count, width))] * (1 + len(parts))
        + [whole_block((width,))],
        out_specs=[whole_block(shape)] * 2,
        out_shape=[jax.ShapeDtypeStruct(shape, jnp.bfloat16)] * 2,
        compiler_params=pltpu.CompilerParams(vmem_limit_bytes=56 << 20),
        cost_estimate=pl.CostEstimate(flops=1, bytes_accessed=1, transcendentals=0),
        name="spread_rows",
    )(place, rows, *parts, gain)


def merge_kernel(place, *refs):
    blocks, (weights, kept, given, rows) = refs[:-4], refs[-4:]
    lines = len(blocks)
    quads = blocks[0].shape[0] // 2
    for index, block in enumerate(blocks):
        base = lax.rem(place[11] + lines - index, lines) * 2
        for half in (0, 1):
            start = (base + (place[9] if half == 0 else 1 - place[9])) * quads
            rows[pl.ds(pl.multiple_of(start, 16), quads), :] = block[half * quads : half * quads + quads]
    wide = jnp.dot(rows[...], weights[...], preferred_element_type=jnp.float32)
    half = kept.shape[1]
    low, high = wide[:, :half], wide[:, half:]
    first_side = place[9] == 0
    kept[...] = jnp.where(first_side, low, high)
    given[...] = jnp.where(first_side, high, low).astype(jnp.bfloat16)


def split_kernel(needed, place, kept, got, *outs):
    for index, out in enumerate(outs):
        for image in range(needed):
            rows = pl.ds(pl.multiple_of(place[TABLE + index * needed + image] * IMG_ROWS, 16), IMG_ROWS)
            both = kept[rows, :] + got[rows, :].astype(jnp.float32)
            out[image * IMG_ROWS : (image + 1) * IMG_ROWS] = both.astype(jnp.bfloat16)


def merge(place, blocks, weights):
    count, size = blocks[0].shape
    rows, half = count * len(blocks), weights.shape[1] // 2
    return pl.pallas_call(
        merge_kernel,
        in_specs=[pl.BlockSpec(memory_space=pltpu.SMEM)]
        + [whole_block((count, size))] * len(blocks)
        + [whole_block(weights.shape)],
        out_specs=[whole_block((rows, half))] * 2,
        out_shape=[
            jax.ShapeDtypeStruct((rows, half), jnp.float32),
            jax.ShapeDtypeStruct((rows, half), jnp.bfloat16),
        ],
        scratch_shapes=[pltpu.VMEM((rows, size), jnp.bfloat16)],
        compiler_params=pltpu.CompilerParams(vmem_limit_bytes=16 << 20),
        cost_estimate=pl.CostEstimate(flops=1, bytes_accessed=1, transcendentals=0),
        name="merge_rows",
    )(place, *blocks, weights)


def after(values, first):
    return lax.optimization_barrier((values, first))[0]


class Queue:
    def __init__(self):
        self.last = []

    def held(self, value):
        return after(value, self.last) if self.last else value

    def passed(self, value):
        self.last = [value]
        return value

    def wait(self, value):
        self.last = self.last + [value]
        return value


def quarter_size(rows):
    return -(-rows // 64) * 16


def quarter_start(rows, index):
    return jnp.minimum(index * quarter_size(rows), rows - quarter_size(rows))


def padded(weights):
    return jnp.pad(weights, ((0, -weights.shape[0] % 16), (0, 0)))


def own_quarter(weights):
    place = lax.axis_index("req") % 4
    size = quarter_size(weights.shape[0])
    return lax.dynamic_slice_in_dim(weights, quarter_start(weights.shape[0], place), size, 0)


def other_copy(values, flip):
    return lax.ppermute(values, "req", [(i, i ^ flip) for i in range(lax.axis_size("req"))])


def line_neighbours(values, tp_size):
    lines = tp_size // 2
    if lines != 4:
        return [turned(values, tp_size, k) for k in range(1, lines)]
    up = lax.ppermute(values, "tp", [(i, i + 2) for i in range(tp_size - 2)])
    down = lax.ppermute(values, "tp", [(i + 2, i) for i in range(tp_size - 2)])
    return [up, turned(values, tp_size, 2), down]


def line_ends(parts, tp_size, queue):
    if tp_size // 2 != 4:
        return parts
    line = lax.axis_index("tp") // 2
    ends = lax.ppermute(queue.held(parts[1]), "tp", [(2, 0), (3, 1), (4, 6), (5, 7)])
    return [jnp.where(line == 0, ends, parts[0]), parts[1], jnp.where(line == 3, ends, parts[2])]


def shards(
    patches, vis_gain, w_fc1, w_fc2, merge_gain, w_merge, slots, text, docs, dec_gain, w_qkv, w_out
):
    patch_rows = patches[0]
    text_rows = text[0]
    width = patch_rows.shape[1]
    seq_here = text_rows.shape[0]
    tp_size = lax.axis_size("tp")
    lines = tp_size // 2
    line = lax.axis_index("tp") // 2
    side = lax.axis_index("tp") % 2

    blk = 2 * seq_here
    longest = seq_here * tp_size // 4
    halo = -(-longest // blk)
    ahead = halo * blk
    window = ahead + blk
    qkv_own = padded(w_qkv.T)
    out_own = padded(w_out)
    columns, depth = qkv_own.shape[0], out_own.shape[0]
    place = lax.axis_index("req") % 4
    starts = jnp.stack(
        [quarter_start(columns, place ^ i) for i in (0, 1, 2, 3)]
        + [quarter_start(depth, place ^ i) for i in (0, 1, 2, 3)]
        + [line * blk - ahead, side, (2 * line + side) * seq_here, line]
    ).astype(jnp.int32)
    bf16 = jnp.bfloat16

    images = slots.shape[1] // IMG_ROWS
    span = seq_here * tp_size // images
    tables = []
    for target in range(lines):
        held = []
        for place_of in range(images):
            low = place_of * span if place_of < images - 1 else images * span - IMG_ROWS
            inside = low < (target + 1) * blk and (place_of + 1) * span > target * blk - ahead
            held.append((not inside, (place_of - images // 2) % images))
        tables.append(sorted(held))
    needed = max(sum(not outside for outside, _ in held) for held in tables)
    table = jnp.array([[image for _, image in held[:needed]] for held in tables], jnp.int32)
    turned_table = table[(line + jnp.arange(lines)) % lines]
    starts = jnp.concatenate([starts, turned_table.reshape(-1)])
    count = needed * IMG_ROWS
    queue = Queue()
    rounds = [k for k in range(1, lines) if k != lines // 2]
    middle = lines // 2
    other, sums, part = {}, {}, {}

    def run_mlp(k, mine):
        own, given = mlp(queue.held(mine), other[k], vis_gain, w_fc1, w_fc2)
        queue.passed((own, given))
        part[k] = own
        return swap_pair(given, tp_size)

    def add_pair(k, got):
        pair = (queue.held(part[k]).astype(jnp.float32) + got.astype(jnp.float32)).astype(bf16)
        queue.passed(pair)
        return turned(pair, tp_size, lines - k)

    swapping = swap_pair(patch_rows, tp_size)
    moving = {k: turned(patch_rows, tp_size, k) for k in rounds + [middle]}
    text_other = swap_pair(text_rows, tp_size)
    other[0] = queue.wait(swapping)
    mine, swapping = {}, {}
    for k in rounds + [middle]:
        mine[k] = queue.wait(moving[k])
    text_other = queue.wait(text_other)
    for k in rounds + [middle]:
        swapping[k] = swap_pair(queue.held(mine[k]), tp_size)
    qkv_quarter, out_quarter = own_quarter(qkv_own), own_quarter(out_own)
    qkv_moving, qkv_ours, qkv_theirs = {}, {}, {}
    place_of = {0: 0, middle: lines - 1, **{k: i + 1 for i, k in enumerate(rounds)}}

    def move_weights(k, part=0, parts=1):
        size = qkv_quarter.shape[0] // parts
        piece = qkv_quarter[part * size : (part + 1) * size]
        qkv_moving.setdefault(k, []).append(turned(queue.held(piece), tp_size, k))

    def cross_weights(k):
        halves = queue.wait(qkv_moving[k])
        qkv_moving[k] = halves[0] if len(halves) == 1 else jnp.concatenate(queue.held(halves))
        qkv_theirs[k] = other_copy(queue.held(qkv_moving[k]), 2)

    def share_weights(k):
        both = jnp.stack([queue.held(qkv_moving[k]), queue.wait(qkv_theirs[k])])
        qkv_ours[k] = queue.passed(both[:, None])
        qkv_theirs[k] = other_copy(qkv_ours[k], 1)

    text_back = []
    for steps_back in range(1, halo + 1):
        steps = [(i, i + 2 * steps_back) for i in range(tp_size - 2 * steps_back)]
        text_back.append(lax.ppermute(queue.held(text_rows), "tp", steps))
    back = {0: run_mlp(0, patch_rows)}
    for index, k in enumerate(rounds):
        other[k] = queue.wait(swapping[k])
        if index == 1:
            text_back = queue.wait(text_back)
            move_weights(middle, 0, 2)
        back[k] = run_mlp(k, mine[k])
    other[middle] = queue.wait(swapping[middle])
    back[middle] = run_mlp(middle, mine[middle])
    queue.wait(qkv_moving[middle][0])
    for k in rounds:
        sums[k] = add_pair(k, queue.wait(back[k]))
    sums[middle] = add_pair(middle, queue.wait(back[middle]))
    move_weights(middle, 1, 2)
    pieces = []
    for rows in text_back[::-1]:
        pieces += [rows, swap_pair(queue.held(rows), tp_size)]
    spread, hits, bias, slots_here = queue.passed(kernel_call(
        functools.partial(mask_kernel, blk, longest), "masks",
        [
            ((count, window), bf16),
            ((8, window), jnp.float32),
            ((blk // 128, longest + 128, 128), jnp.float32),
            ((8, count), jnp.int32),
        ],
        starts, queue.held(slots), docs,
    ))
    sums[0] = part[0]
    sums = [queue.wait(back[0])] + [queue.wait(sums[k]) for k in range(lines)]
    cross_weights(middle)
    kept, given = queue.passed(
        spread_rows(starts, queue.held(patch_rows), sums, merge_gain, lines)
    )
    got = swap_pair(queue.held(given), tp_size)
    move_weights(rounds[0])
    pieces = queue.wait(pieces) + [text_rows, text_other]
    text_normed, text_parts = queue.passed(kernel_call(
        text_kernel, "text_first", [((window, width), bf16), ((lines, columns, window), bf16)],
        starts, queue.held(dec_gain), qkv_own, *pieces,
        grid=(1,),
        out_specs=[
            whole_block((window, width)),
            pl.BlockSpec((1, columns, window), lambda _: (0, 0, 0)),
        ],
    ))

    def run_text(text_parts, k):
        return queue.passed(kernel_call(
            text_next_kernel, "text_next", [((lines, columns, window), bf16)],
            starts, queue.held(text_normed), qkv_ours[k], queue.wait(qkv_theirs[k]), text_parts,
            grid=(window // 256,),
            specs={
                1: pl.BlockSpec((256, width), lambda i: (i, 0)),
                4: pl.BlockSpec(memory_space=pl.ANY),
            },
            out_specs=[pl.BlockSpec((1, columns, 256), lambda i: (place_of[k], 0, i))],
            scratch=[pltpu.VMEM((columns, width), bf16)],
            aliases={4: 0},
        ))[0]

    got = queue.wait(got)
    cross_weights(rounds[0])
    share_weights(middle)
    blocks = queue.passed([jnp.concatenate([queue.held(kept[k]), got[k]]) for k in range(lines)])
    blocks = [blocks[0]] + [turned(blocks[k], tp_size, k) for k in range(1, lines)]
    queue.wait(blocks)
    kept, given = queue.passed(merge(starts, [queue.held(blocks[0])] + blocks[1:], w_merge))
    half = kept.shape[1]
    got = swap_pair(given, tp_size)
    for k in rounds[1:]:
        move_weights(k)
    text_parts = run_text(text_parts, middle)
    got = queue.wait(got)
    for k in rounds[1:]:
        cross_weights(k)
    share_weights(rounds[0])
    share = queue.passed(kernel_call(
        functools.partial(split_kernel, needed), "image_shares", [((count, half), bf16)] * lines,
        starts, queue.held(kept), got,
    ))
    moving = [turned(share[k], tp_size, k) for k in range(1, lines)]
    text_parts = run_text(text_parts, rounds[0])
    total = queue.held(share[0]).astype(jnp.float32)
    for block in queue.wait(moving):
        total = total + block.astype(jnp.float32)
    total = queue.passed(total.astype(bf16))
    for k in rounds[1:]:
        share_weights(k)
    far = swap_pair(queue.held(total), tp_size)
    out_moving = [turned(queue.held(out_quarter), tp_size, k) for k in rounds + [middle]]
    for k in rounds[1:]:
        text_parts = run_text(text_parts, k)
    merged, image_rows = queue.passed(kernel_call(
        image_rows_kernel, "image_rows", [((count, width), bf16)] * 2,
        starts, queue.held(total), queue.wait(far), dec_gain,
    ))
    line_pieces = [x[k] for k in rounds + [middle] for x in (qkv_ours, qkv_theirs)]
    sources = [text_parts, qkv_own] + line_pieces
    out_near = queue.passed(jnp.stack(queue.wait([queue.held(part) for part in out_moving])))
    out_far = other_copy(out_near, 2)
    kept, given = queue.passed(kernel_call(
        functools.partial(late_kernel, blk, longest, lines, depth), "late_attention",
        [((seq_here, lines * depth), bf16)] * 2,
        starts, queue.held(image_rows), spread, hits, bias, *sources,
        specs={5 + i: pl.BlockSpec(memory_space=pl.ANY) for i in range(2 * lines)},
        scratch=[pltpu.VMEM(source.shape, bf16) for source in sources] + [
            pltpu.VMEM((columns, width), bf16),
            pltpu.VMEM((lines * depth, blk), jnp.float32),
            pltpu.SemaphoreType.DMA((3 * lines,)),
        ],
    ))
    out_ours = queue.passed(jnp.stack([queue.held(out_near), queue.wait(out_far)]))
    out_theirs = other_copy(out_ours, 1)
    (given,) = queue.passed(project(starts, queue.held(given), out_own, out_ours, queue.wait(out_theirs)))
    got = swap_pair(given, tp_size)
    (kept,) = queue.passed(project(starts, queue.held(kept), out_own, out_ours, out_theirs))
    (decoded,) = kernel_call(
        out_kernel, "out_rows", [((seq_here, width), bf16)],
        starts, queue.held(text_rows), slots_here, merged, kept, queue.wait(got),
    )
    return decoded[None]


def solution(mesh):
    placed = (
        P("req", "tp", None),
        P(),
        P(None, "tp"),
        P("tp", None),
        P(),
        P("tp", None),
        P("req", None),
        P("req", "tp", None),
        P("req", None),
        P(),
        P(None, "tp"),
        P("tp", None),
    )
    return jax.shard_map(
        shards, mesh=mesh, in_specs=placed, out_specs=P("req", "tp", None), check_vma=False
    )
```

```python
import functools
import math

import jax
import jax.numpy as jnp
from jax import lax
from jax.experimental import pallas as pl
from jax.experimental.pallas import tpu as pltpu
from jax.sharding import PartitionSpec as P

HD = 104
IMG_ROWS = 64
TABLE = 12


EPSILON = 1e-06


def layer_norm(values, gains):
    average = jnp.mean(values, axis=-1, keepdims=True)
    centred = values - average
    variance = jnp.mean(centred * centred, axis=-1, keepdims=True)
    return centred * lax.rsqrt(variance + EPSILON) * gains


def rms_norm(values, gains):
    return values * lax.rsqrt(jnp.mean(values * values, axis=-1, keepdims=True) + EPSILON) * gains


def pair_steps(tp_size):
    return [(i, i ^ 1) for i in range(tp_size)]


def turn_steps(tp_size, turn):
    lines = tp_size // 2
    return [(a * 2 + b, ((a + turn) % lines) * 2 + b) for a in range(lines) for b in range(2)]


def swap_pair(values, tp_size):
    return lax.ppermute(values, "tp", pair_steps(tp_size))


def turned(values, tp_size, turn):
    return lax.ppermute(values, "tp", turn_steps(tp_size, turn))


NT = (((1,), (1,)), ((), ()))
TN = (((0,), (0,)), ((), ()))


def put_quarters(whole, ours, theirs, starts, offset):
    size = ours.shape[2]
    for index in range(4):
        quarter = ours[index // 2, 0] if index % 2 == 0 else theirs[index // 2, 0]
        start = pl.multiple_of(starts[offset + index], 16)
        whole[pl.ds(start, size), :] = quarter


def text_kernel(starts, gain, own, *refs):
    pieces, (rows, out) = refs[:-2], refs[-2:]
    count = pieces[0].shape[0]
    first_side = starts[9] == 0
    for index in range(0, len(pieces), 2):
        mine, other = pieces[index][...], pieces[index + 1][...]
        both = (jnp.where(first_side, mine, other), jnp.where(first_side, other, mine))
        for half, part in enumerate(both):
            normed = rms_norm(part.astype(jnp.float32), gain[...].reshape(1, -1))
            rows[pl.ds((index + half) * count, count), :] = normed.astype(jnp.bfloat16)
    out[0] = lax.dot_general(
        own[...], rows[...], NT, preferred_element_type=jnp.float32
    ).astype(jnp.bfloat16)


def text_next_kernel(starts, rows, ours, theirs, before, out, whole):
    @pl.when(pl.program_id(0) == 0)
    def _():
        put_quarters(whole, ours, theirs, starts, 0)

    out[0] = lax.dot_general(
        whole[...], rows[...], NT, preferred_element_type=jnp.float32
    ).astype(jnp.bfloat16)


def mask_kernel(blk, longest, starts, slots, docs, spread, hits, bias, slots_here):
    count, window = spread.shape
    ahead = window - blk
    for index in range(count // IMG_ROWS):
        picked = slots[:, :IMG_ROWS]
        for image in range(1, slots.shape[1] // IMG_ROWS):
            rows = slots[:, image * IMG_ROWS : (image + 1) * IMG_ROWS]
            picked = jnp.where(starts[TABLE + index] == image, rows, picked)
        slots_here[:, index * IMG_ROWS : (index + 1) * IMG_ROWS] = jnp.broadcast_to(
            picked, (8, IMG_ROWS)
        )
    slot_columns = jnp.broadcast_to(slots_here[0:1, :].astype(jnp.float32), (128, count)).T
    position = starts[8] + lax.broadcasted_iota(jnp.int32, spread.shape, 1)
    match = jnp.where(slot_columns[:, 0:1] == position.astype(jnp.float32), 1.0, 0.0)
    spread[...] = match.astype(jnp.bfloat16)
    hits[...] = jnp.broadcast_to(jnp.max(match, axis=0, keepdims=True), hits.shape)
    line = starts[11]
    parts = []
    for back in range(ahead // blk, -1, -1):
        start = pl.multiple_of(jnp.maximum(line - back, 0) * blk, 128)
        part = docs[:, pl.ds(start, blk)].astype(jnp.float32)
        parts.append(jnp.where(line >= back, part, -1.0))
    doc_row = jnp.concatenate(parts, axis=1)
    doc_columns = jnp.broadcast_to(doc_row, (128, window)).T
    reach = longest + 128
    for block in range(blk // 128):
        first = ahead - longest + block * 128
        key_place = first + lax.broadcasted_iota(jnp.int32, (reach, 128), 0)
        query_place = ahead + block * 128 + lax.broadcasted_iota(jnp.int32, (reach, 128), 1)
        query_docs = doc_row[:, ahead + block * 128 : ahead + block * 128 + 128]
        allowed = (key_place <= query_place) & (doc_columns[first : first + reach] == query_docs)
        bias[block] = jnp.where(allowed, 0.0, -1e30)


def image_rows_kernel(starts, ours, theirs, gain, merged, normed):
    first_side = starts[9] == 0
    mine, other = ours[...], theirs[...]
    merged[...] = jnp.concatenate(
        [jnp.where(first_side, mine, other), jnp.where(first_side, other, mine)], axis=1
    )
    normed[...] = rms_norm(merged[...].astype(jnp.float32), gain[...].reshape(1, -1)).astype(jnp.bfloat16)


def late_kernel(blk, longest, lines, depth, starts, image_rows, spread, hits, bias, *refs):
    sources, near = refs[: 2 * lines], refs[2 * lines + 2 : 4 * lines + 2]
    kept, given = refs[2 * lines : 2 * lines + 2]
    whole, blended, arrived = refs[-3:]
    texts, text_near = sources[0], near[0]
    copies = [pltpu.make_async_copy(texts.at[0], text_near.at[0], arrived.at[0])]
    copies.append(pltpu.make_async_copy(sources[1], near[1], arrived.at[1]))
    for line in range(1, lines):
        for place in (2 * line, 2 * line + 1):
            copies.append(pltpu.make_async_copy(sources[place], near[place], arrived.at[place]))
        copies.append(
            pltpu.make_async_copy(texts.at[line], text_near.at[line], arrived.at[2 * lines + line])
        )
    for copy in copies:
        copy.start()
    ahead = spread.shape[1] - blk
    reach = longest + 128
    factor = math.log2(math.e) / math.sqrt(HD)
    hit = hits[0:1, :] > 0.5
    heads = near[1].shape[0] // (3 * HD)
    if heads * HD < depth:
        blended[...] = jnp.zeros_like(blended)
    for line in range(lines):
        for copy in copies[: 2] if line == 0 else copies[3 * line - 1 : 3 * line + 2]:
            copy.wait()
        if line:
            put_quarters(whole, near[2 * line], near[2 * line + 1], starts, 0)
        weights = whole if line else near[1]
        image_part = lax.dot_general(
            image_rows[...], weights[...], NT, preferred_element_type=jnp.float32
        ).astype(jnp.bfloat16)
        placed = lax.dot_general(
            image_part, spread[...], TN, preferred_element_type=jnp.float32
        )
        for head in range(heads):
            base = head * 3 * HD

            def picked(part, start):
                rows = pl.ds(base + part * HD, HD)
                image = placed[base + part * HD : base + (part + 1) * HD, start:]
                text = text_near[line, rows, start:].astype(jnp.float32)
                return jnp.where(hit[:, start:], image, text)

            queries = (picked(0, ahead) * factor).astype(jnp.bfloat16)
            keys = picked(1, 0).T.astype(jnp.bfloat16)
            values = picked(2, 0).astype(jnp.bfloat16)
            blocks = range(blk // 128)
            firsts = [ahead - longest + block * 128 for block in blocks]
            scores = [
                jnp.dot(
                    keys[first : first + reach],
                    queries[:, block * 128 : block * 128 + 128],
                    preferred_element_type=jnp.float32,
                ) + bias[block]
                for block, first in zip(blocks, firsts)
            ]
            raised = [jnp.exp2(part - jnp.max(part, axis=0, keepdims=True)) for part in scores]
            shares = [1.0 / jnp.sum(part, axis=0, keepdims=True) for part in raised]
            mixed = [
                jnp.dot(
                    values[:, first : first + reach],
                    part.astype(jnp.bfloat16),
                    preferred_element_type=jnp.float32,
                )
                for first, part in zip(firsts, raised)
            ]
            for block in blocks:
                columns = pl.ds(block * 128, 128)
                blended[pl.ds(line * depth + head * HD, HD), columns] = mixed[block] * shares[block]
    attended = blended[...].T.astype(jnp.bfloat16)
    low, high = attended[: blk // 2], attended[blk // 2 :]
    first_side = starts[9] == 0
    kept[...] = jnp.where(first_side, low, high)
    given[...] = jnp.where(first_side, high, low)


def project_kernel(starts, rows, own, ours, theirs, out, whole):
    depth = own.shape[0]
    whole[:depth] = own[...]
    size = ours.shape[2]
    for line in range(ours.shape[1]):
        for index in range(4):
            quarter = (ours if index % 2 == 0 else theirs)[index // 2, line]
            start = pl.multiple_of((line + 1) * depth + starts[4 + index], 16)
            whole[pl.ds(start, size), :] = quarter
    total = jnp.dot(rows[...], whole[...], preferred_element_type=jnp.float32)
    out[...] = total.astype(jnp.bfloat16)


def out_kernel(starts, text, slots, merged, kept, out):
    count = text.shape[0]
    position = starts[10] + lax.broadcasted_iota(jnp.int32, (count, merged.shape[0]), 0)
    match = jnp.where(slots[0:1, :] == position, 1.0, 0.0)
    placed = jnp.dot(match.astype(jnp.bfloat16), merged[...], preferred_element_type=jnp.float32)
    hit = jnp.max(match, axis=1, keepdims=True) > 0.5
    embedded = jnp.where(hit, placed, text[...].astype(jnp.float32))
    out[...] = embedded + kept[...].astype(jnp.float32)


SMEM = pl.BlockSpec(memory_space=pltpu.SMEM)


def kernel_call(body, name, results, *operands, scratch=(), grid=(), specs={}, out_specs=None, aliases={}):
    return pl.pallas_call(
        body,
        grid=grid,
        in_specs=[SMEM]
        + [
            specs.get(place, whole_block(value.shape))
            for place, value in enumerate(operands)
            if place
        ],
        out_specs=out_specs or [whole_block(shape) for shape, _ in results],
        out_shape=[jax.ShapeDtypeStruct(shape, dtype) for shape, dtype in results],
        scratch_shapes=list(scratch),
        input_output_aliases=aliases,
        compiler_params=pltpu.CompilerParams(vmem_limit_bytes=56 << 20),
        cost_estimate=pl.CostEstimate(flops=1, bytes_accessed=1, transcendentals=0),
        name=name,
    )(*operands)


def quarters_spec(values, line_of):
    shape = (2, 1) + values.shape[2:]
    return pl.BlockSpec(shape, lambda k: (0, line_of(k), 0, 0))


def project(starts, rows, own, ours, theirs):
    lines = ours.shape[1] + 1
    return kernel_call(
        project_kernel, "project", [((rows.shape[0], own.shape[1]), jnp.bfloat16)],
        starts, rows, own, ours, theirs,
        scratch=[pltpu.VMEM((lines * own.shape[0], own.shape[1]), jnp.bfloat16)],
    )


def mlp_kernel(mine, other, gain, w_in, w_back, out_mine, out_other, rows, total):
    step = pl.program_id(0)
    count = mine.shape[0]

    @pl.when(step == 0)
    def _():
        for place, part in ((0, mine), (count, other)):
            normed = layer_norm(part[...].astype(jnp.float32), gain[...].reshape(1, -1))
            rows[pl.ds(place, count), :] = normed.astype(jnp.bfloat16)
        total[...] = jnp.zeros_like(total)

    wide = jnp.dot(rows[...], w_in[...], preferred_element_type=jnp.float32)
    hidden = 0.5 * wide * (1.0 + lax.erf(wide * math.sqrt(0.5)))
    total[...] += jnp.dot(
        hidden.astype(jnp.bfloat16), w_back[...], preferred_element_type=jnp.float32
    )

    @pl.when(step == pl.num_programs(0) - 1)
    def _():
        out_mine[...] = total[:count].astype(jnp.bfloat16)
        out_other[...] = total[count:].astype(jnp.bfloat16)


def whole_block(shape):
    return pl.BlockSpec(shape, lambda *_: (0,) * len(shape))


def mlp(mine, other, gain, w_in, w_back):
    count, width = mine.shape
    units = w_in.shape[1]
    step = 256
    return pl.pallas_call(
        mlp_kernel,
        grid=(units // step,),
        in_specs=[
            whole_block((count, width)),
            whole_block((count, width)),
            whole_block((width,)),
            pl.BlockSpec((width, step), lambda i: (0, i)),
            pl.BlockSpec((step, width), lambda i: (i, 0)),
        ],
        out_specs=[whole_block((count, width))] * 2,
        out_shape=[jax.ShapeDtypeStruct((count, width), jnp.bfloat16)] * 2,
        scratch_shapes=[
            pltpu.VMEM((2 * count, width), jnp.bfloat16),
            pltpu.VMEM((2 * count, width), jnp.float32),
        ],
        compiler_params=pltpu.CompilerParams(vmem_limit_bytes=16 << 20),
        cost_estimate=pl.CostEstimate(flops=1, bytes_accessed=1, transcendentals=0),
        name="mlp_rows",
    )(mine, other, gain, w_in, w_back)


def spread_kernel(lines, place, rows, *refs):
    parts, (gain, kept, given) = refs[:-3], refs[-3:]
    wide = rows[...].astype(jnp.float32)
    for part in parts:
        wide = wide + part[...].astype(jnp.float32)
    normed = layer_norm(wide, gain[...].reshape(1, -1)).astype(jnp.bfloat16)
    size = kept.shape[2]
    quads = kept.shape[1]
    to = lax.broadcasted_iota(jnp.int32, (4 * quads, 4 * quads), 0)
    by = lax.broadcasted_iota(jnp.int32, (4 * quads, 4 * quads), 1)
    moves = jnp.where(by == to % quads * 4 + to // quads, 1.0, 0.0).astype(jnp.bfloat16)
    sorted_rows = jnp.dot(moves, normed, preferred_element_type=jnp.float32).astype(jnp.bfloat16)
    first_side = place[9] == 0
    for target in range(lines):
        row, base = target // (lines // 4), target % (lines // 4) * 2 * size
        picked = sorted_rows[row * quads : (row + 1) * quads]
        low, high = picked[:, base : base + size], picked[:, base + size : base + 2 * size]
        turn = lax.rem(target + lines - place[11], lines)
        kept[turn] = jnp.where(first_side, low, high)
        given[turn] = jnp.where(first_side, high, low)


def spread_rows(place, rows, parts, gain, lines):
    count, width = rows.shape
    shape = (lines, count // 4, 2 * width // lines)
    return pl.pallas_call(
        functools.partial(spread_kernel, lines),
        in_specs=[pl.BlockSpec(memory_space=pltpu.SMEM)]
        + [whole_block((count, width))] * (1 + len(parts))
        + [whole_block((width,))],
        out_specs=[whole_block(shape)] * 2,
        out_shape=[jax.ShapeDtypeStruct(shape, jnp.bfloat16)] * 2,
        compiler_params=pltpu.CompilerParams(vmem_limit_bytes=56 << 20),
        cost_estimate=pl.CostEstimate(flops=1, bytes_accessed=1, transcendentals=0),
        name="spread_rows",
    )(place, rows, *parts, gain)


def merge_kernel(place, *refs):
    blocks, (weights, kept, given, rows) = refs[:-4], refs[-4:]
    lines = len(blocks)
    quads = blocks[0].shape[0] // 2
    for index, block in enumerate(blocks):
        base = lax.rem(place[11] + lines - index, lines) * 2
        for half in (0, 1):
            start = (base + (place[9] if half == 0 else 1 - place[9])) * quads
            rows[pl.ds(pl.multiple_of(start, 16), quads), :] = block[half * quads : half * quads + quads]
    wide = jnp.dot(rows[...], weights[...], preferred_element_type=jnp.float32)
    half = kept.shape[1]
    low, high = wide[:, :half], wide[:, half:]
    first_side = place[9] == 0
    kept[...] = jnp.where(first_side, low, high)
    given[...] = jnp.where(first_side, high, low).astype(jnp.bfloat16)


def split_kernel(needed, place, kept, got, *outs):
    for index, out in enumerate(outs):
        for image in range(needed):
            rows = pl.ds(pl.multiple_of(place[TABLE + index * needed + image] * IMG_ROWS, 16), IMG_ROWS)
            both = kept[rows, :] + got[rows, :].astype(jnp.float32)
            out[image * IMG_ROWS : (image + 1) * IMG_ROWS] = both.astype(jnp.bfloat16)


def merge(place, blocks, weights):
    count, size = blocks[0].shape
    rows, half = count * len(blocks), weights.shape[1] // 2
    return pl.pallas_call(
        merge_kernel,
        in_specs=[pl.BlockSpec(memory_space=pltpu.SMEM)]
        + [whole_block((count, size))] * len(blocks)
        + [whole_block(weights.shape)],
        out_specs=[whole_block((rows, half))] * 2,
        out_shape=[
            jax.ShapeDtypeStruct((rows, half), jnp.float32),
            jax.ShapeDtypeStruct((rows, half), jnp.bfloat16),
        ],
        scratch_shapes=[pltpu.VMEM((rows, size), jnp.bfloat16)],
        compiler_params=pltpu.CompilerParams(vmem_limit_bytes=16 << 20),
        cost_estimate=pl.CostEstimate(flops=1, bytes_accessed=1, transcendentals=0),
        name="merge_rows",
    )(place, *blocks, weights)


def after(values, first):
    return lax.optimization_barrier((values, first))[0]


class Queue:
    def __init__(self):
        self.last = []

    def held(self, value):
        return after(value, self.last) if self.last else value

    def passed(self, value):
        self.last = [value]
        return value

    def wait(self, value):
        self.last = self.last + [value]
        return value


def quarter_size(rows):
    return -(-rows // 64) * 16


def quarter_start(rows, index):
    return jnp.minimum(index * quarter_size(rows), rows - quarter_size(rows))


def padded(weights):
    return jnp.pad(weights, ((0, -weights.shape[0] % 16), (0, 0)))


def own_quarter(weights):
    place = lax.axis_index("req") % 4
    size = quarter_size(weights.shape[0])
    return lax.dynamic_slice_in_dim(weights, quarter_start(weights.shape[0], place), size, 0)


def other_copy(values, flip):
    return lax.ppermute(values, "req", [(i, i ^ flip) for i in range(lax.axis_size("req"))])


def line_neighbours(values, tp_size):
    lines = tp_size // 2
    if lines != 4:
        return [turned(values, tp_size, k) for k in range(1, lines)]
    up = lax.ppermute(values, "tp", [(i, i + 2) for i in range(tp_size - 2)])
    down = lax.ppermute(values, "tp", [(i + 2, i) for i in range(tp_size - 2)])
    return [up, turned(values, tp_size, 2), down]


def line_ends(parts, tp_size, queue):
    if tp_size // 2 != 4:
        return parts
    line = lax.axis_index("tp") // 2
    ends = lax.ppermute(queue.held(parts[1]), "tp", [(2, 0), (3, 1), (4, 6), (5, 7)])
    return [jnp.where(line == 0, ends, parts[0]), parts[1], jnp.where(line == 3, ends, parts[2])]


def shards(
    patches, vis_gain, w_fc1, w_fc2, merge_gain, w_merge, slots, text, docs, dec_gain, w_qkv, w_out
):
    patch_rows = patches[0]
    text_rows = text[0]
    width = patch_rows.shape[1]
    seq_here = text_rows.shape[0]
    tp_size = lax.axis_size("tp")
    lines = tp_size // 2
    line = lax.axis_index("tp") // 2
    side = lax.axis_index("tp") % 2

    blk = 2 * seq_here
    longest = seq_here * tp_size // 4
    halo = -(-longest // blk)
    ahead = halo * blk
    window = ahead + blk
    qkv_own = padded(w_qkv.T)
    out_own = padded(w_out)
    columns, depth = qkv_own.shape[0], out_own.shape[0]
    place = lax.axis_index("req") % 4
    starts = jnp.stack(
        [quarter_start(columns, place ^ i) for i in (0, 1, 2, 3)]
        + [quarter_start(depth, place ^ i) for i in (0, 1, 2, 3)]
        + [line * blk - ahead, side, (2 * line + side) * seq_here, line]
    ).astype(jnp.int32)
    bf16 = jnp.bfloat16

    images = slots.shape[1] // IMG_ROWS
    span = seq_here * tp_size // images
    tables = []
    for target in range(lines):
        held = []
        for place_of in range(images):
            low = place_of * span if place_of < images - 1 else images * span - IMG_ROWS
            inside = low < (target + 1) * blk and (place_of + 1) * span > target * blk - ahead
            held.append((not inside, (place_of - images // 2) % images))
        tables.append(sorted(held))
    needed = max(sum(not outside for outside, _ in held) for held in tables)
    table = jnp.array([[image for _, image in held[:needed]] for held in tables], jnp.int32)
    turned_table = table[(line + jnp.arange(lines)) % lines]
    starts = jnp.concatenate([starts, turned_table.reshape(-1)])
    count = needed * IMG_ROWS
    queue = Queue()
    rounds = [k for k in range(1, lines) if k != lines // 2]
    middle = lines // 2
    other, sums, part = {}, {}, {}

    def run_mlp(k, mine):
        own, given = mlp(queue.held(mine), other[k], vis_gain, w_fc1, w_fc2)
        queue.passed((own, given))
        part[k] = own
        return swap_pair(given, tp_size)

    def add_pair(k, got):
        pair = (queue.held(part[k]).astype(jnp.float32) + got.astype(jnp.float32)).astype(bf16)
        queue.passed(pair)
        return turned(pair, tp_size, lines - k)

    swapping = swap_pair(patch_rows, tp_size)
    moving = {k: turned(patch_rows, tp_size, k) for k in rounds + [middle]}
    text_other = swap_pair(text_rows, tp_size)
    qkv_quarter, out_quarter = queue.passed((own_quarter(qkv_own), own_quarter(out_own)))
    other[0] = queue.wait(swapping)
    mine, swapping = {}, {}
    for k in rounds + [middle]:
        mine[k] = queue.wait(moving[k])
    text_other = queue.wait(text_other)
    for k in rounds + [middle]:
        swapping[k] = swap_pair(queue.held(mine[k]), tp_size)
    qkv_moving, qkv_ours, qkv_theirs = {}, {}, {}
    place_of = {0: 0, middle: lines - 1, **{k: i + 1 for i, k in enumerate(rounds)}}

    def move_weights(k, part=0, parts=1):
        size = qkv_quarter.shape[0] // parts
        piece = qkv_quarter[part * size : (part + 1) * size]
        qkv_moving.setdefault(k, []).append(turned(queue.held(piece), tp_size, k))

    def cross_weights(k):
        halves = queue.wait(qkv_moving[k])
        qkv_moving[k] = halves[0] if len(halves) == 1 else jnp.concatenate(queue.held(halves))
        qkv_theirs[k] = other_copy(queue.held(qkv_moving[k]), 2)

    def share_weights(k):
        both = jnp.stack([queue.held(qkv_moving[k]), queue.wait(qkv_theirs[k])])
        qkv_ours[k] = queue.passed(both[:, None])
        qkv_theirs[k] = other_copy(qkv_ours[k], 1)

    text_back = []
    for steps_back in range(1, halo + 1):
        steps = [(i, i + 2 * steps_back) for i in range(tp_size - 2 * steps_back)]
        text_back.append(lax.ppermute(queue.held(text_rows), "tp", steps))
    back = {0: run_mlp(0, patch_rows)}
    for index, k in enumerate(rounds):
        other[k] = queue.wait(swapping[k])
        if index == 1:
            text_back = queue.wait(text_back)
            move_weights(middle, 0, 2)
        back[k] = run_mlp(k, mine[k])
    other[middle] = queue.wait(swapping[middle])
    back[middle] = run_mlp(middle, mine[middle])
    queue.wait(qkv_moving[middle][0])
    for k in rounds:
        sums[k] = add_pair(k, queue.wait(back[k]))
    sums[middle] = add_pair(middle, queue.wait(back[middle]))
    move_weights(middle, 1, 2)
    pieces = []
    for rows in text_back[::-1]:
        pieces += [rows, swap_pair(queue.held(rows), tp_size)]
    spread, hits, bias, slots_here = queue.passed(kernel_call(
        functools.partial(mask_kernel, blk, longest), "masks",
        [
            ((count, window), bf16),
            ((8, window), jnp.float32),
            ((blk // 128, longest + 128, 128), jnp.float32),
            ((8, count), jnp.int32),
        ],
        starts, queue.held(slots), docs,
    ))
    sums[0] = part[0]
    sums = [queue.wait(back[0])] + [queue.wait(sums[k]) for k in range(lines)]
    cross_weights(middle)
    kept, given = queue.passed(
        spread_rows(starts, queue.held(patch_rows), sums, merge_gain, lines)
    )
    got = swap_pair(queue.held(given), tp_size)
    move_weights(rounds[0])
    pieces = queue.wait(pieces) + [text_rows, text_other]
    text_normed, text_parts = queue.passed(kernel_call(
        text_kernel, "text_first", [((window, width), bf16), ((lines, columns, window), bf16)],
        starts, queue.held(dec_gain), qkv_own, *pieces,
        grid=(1,),
        out_specs=[
            whole_block((window, width)),
            pl.BlockSpec((1, columns, window), lambda _: (0, 0, 0)),
        ],
    ))

    def run_text(text_parts, k):
        return queue.passed(kernel_call(
            text_next_kernel, "text_next", [((lines, columns, window), bf16)],
            starts, queue.held(text_normed), qkv_ours[k], queue.wait(qkv_theirs[k]), text_parts,
            grid=(window // 256,),
            specs={
                1: pl.BlockSpec((256, width), lambda i: (i, 0)),
                4: pl.BlockSpec(memory_space=pl.ANY),
            },
            out_specs=[pl.BlockSpec((1, columns, 256), lambda i: (place_of[k], 0, i))],
            scratch=[pltpu.VMEM((columns, width), bf16)],
            aliases={4: 0},
        ))[0]

    got = queue.wait(got)
    cross_weights(rounds[0])
    share_weights(middle)
    blocks = queue.passed([jnp.concatenate([queue.held(kept[k]), got[k]]) for k in range(lines)])
    blocks = [blocks[0]] + [turned(blocks[k], tp_size, k) for k in range(1, lines)]
    queue.wait(blocks)
    kept, given = queue.passed(merge(starts, [queue.held(blocks[0])] + blocks[1:], w_merge))
    half = kept.shape[1]
    got = swap_pair(given, tp_size)
    for k in rounds[1:]:
        move_weights(k)
    text_parts = run_text(text_parts, middle)
    got = queue.wait(got)
    share = queue.passed(kernel_call(
        functools.partial(split_kernel, needed), "image_shares", [((count, half), bf16)] * lines,
        starts, queue.held(kept), got,
    ))
    moving = [turned(share[k], tp_size, k) for k in range(1, lines)]
    for k in rounds[1:]:
        cross_weights(k)
    share_weights(rounds[0])
    text_parts = run_text(text_parts, rounds[0])
    total = queue.held(share[0]).astype(jnp.float32)
    for block in queue.wait(moving):
        total = total + block.astype(jnp.float32)
    total = queue.passed(total.astype(bf16))
    for k in rounds[1:]:
        share_weights(k)
    far = swap_pair(queue.held(total), tp_size)
    out_moving = [turned(queue.held(out_quarter), tp_size, k) for k in rounds + [middle]]
    for k in rounds[1:]:
        text_parts = run_text(text_parts, k)
    merged, image_rows = queue.passed(kernel_call(
        image_rows_kernel, "image_rows", [((count, width), bf16)] * 2,
        starts, queue.held(total), queue.wait(far), dec_gain,
    ))
    line_pieces = [x[k] for k in rounds + [middle] for x in (qkv_ours, qkv_theirs)]
    sources = [text_parts, qkv_own] + line_pieces
    out_near = queue.passed(jnp.stack(queue.wait([queue.held(part) for part in out_moving])))
    out_far = other_copy(out_near, 2)
    kept, given = queue.passed(kernel_call(
        functools.partial(late_kernel, blk, longest, lines, depth), "late_attention",
        [((seq_here, lines * depth), bf16)] * 2,
        starts, queue.held(image_rows), spread, hits, bias, *sources,
        specs={5 + i: pl.BlockSpec(memory_space=pl.ANY) for i in range(2 * lines)},
        scratch=[pltpu.VMEM(source.shape, bf16) for source in sources] + [
            pltpu.VMEM((columns, width), bf16),
            pltpu.VMEM((lines * depth, blk), jnp.float32),
            pltpu.SemaphoreType.DMA((3 * lines,)),
        ],
    ))
    out_ours = queue.passed(jnp.stack([queue.held(out_near), queue.wait(out_far)]))
    out_theirs = other_copy(out_ours, 1)
    (given,) = queue.passed(project(starts, queue.held(given), out_own, out_ours, queue.wait(out_theirs)))
    got = swap_pair(given, tp_size)
    (kept,) = queue.passed(project(starts, queue.held(kept), out_own, out_ours, out_theirs))
    (own_rows,) = queue.passed(kernel_call(
        out_kernel, "out_rows", [((seq_here, width), jnp.float32)],
        starts, queue.held(text_rows), slots_here, merged, kept,
    ))
    decoded = (queue.held(own_rows) + queue.wait(got).astype(jnp.float32)).astype(bf16)
    return decoded[None]


def solution(mesh):
    placed = (
        P("req", "tp", None),
        P(),
        P(None, "tp"),
        P("tp", None),
        P(),
        P("tp", None),
        P("req", None),
        P("req", "tp", None),
        P("req", None),
        P(),
        P(None, "tp"),
        P("tp", None),
    )
    return jax.shard_map(
        shards, mesh=mesh, in_specs=placed, out_specs=P("req", "tp", None), check_vma=False
    )
```

```python
import functools
import math

import jax
import jax.numpy as jnp
from jax import lax
from jax.experimental import pallas as pl
from jax.experimental.pallas import tpu as pltpu
from jax.sharding import PartitionSpec as P

HD = 104
IMG_ROWS = 64
TABLE = 12


EPSILON = 1e-06


def layer_norm(values, gains):
    average = jnp.mean(values, axis=-1, keepdims=True)
    centred = values - average
    variance = jnp.mean(centred * centred, axis=-1, keepdims=True)
    return centred * lax.rsqrt(variance + EPSILON) * gains


def rms_norm(values, gains):
    return values * lax.rsqrt(jnp.mean(values * values, axis=-1, keepdims=True) + EPSILON) * gains


def pair_steps(tp_size):
    return [(i, i ^ 1) for i in range(tp_size)]


def turn_steps(tp_size, turn):
    lines = tp_size // 2
    return [(a * 2 + b, ((a + turn) % lines) * 2 + b) for a in range(lines) for b in range(2)]


def swap_pair(values, tp_size):
    return lax.ppermute(values, "tp", pair_steps(tp_size))


def turned(values, tp_size, turn):
    return lax.ppermute(values, "tp", turn_steps(tp_size, turn))


NT = (((1,), (1,)), ((), ()))
TN = (((0,), (0,)), ((), ()))


def put_quarters(whole, ours, theirs, starts, offset):
    size = ours.shape[2]
    for index in range(4):
        quarter = ours[index // 2, 0] if index % 2 == 0 else theirs[index // 2, 0]
        start = pl.multiple_of(starts[offset + index], 16)
        whole[pl.ds(start, size), :] = quarter


def text_kernel(starts, gain, own, *refs):
    pieces, (rows, out) = refs[:-2], refs[-2:]
    count = pieces[0].shape[0]
    first_side = starts[9] == 0
    for index in range(0, len(pieces), 2):
        mine, other = pieces[index][...], pieces[index + 1][...]
        both = (jnp.where(first_side, mine, other), jnp.where(first_side, other, mine))
        for half, part in enumerate(both):
            normed = rms_norm(part.astype(jnp.float32), gain[...].reshape(1, -1))
            rows[pl.ds((index + half) * count, count), :] = normed.astype(jnp.bfloat16)
    out[0] = lax.dot_general(
        own[...], rows[...], NT, preferred_element_type=jnp.float32
    ).astype(jnp.bfloat16)


def text_next_kernel(starts, rows, ours, theirs, before, out, whole):
    @pl.when(pl.program_id(0) == 0)
    def _():
        put_quarters(whole, ours, theirs, starts, 0)

    out[0] = lax.dot_general(
        whole[...], rows[...], NT, preferred_element_type=jnp.float32
    ).astype(jnp.bfloat16)


def mask_kernel(blk, longest, starts, slots, docs, spread, hits, bias, slots_here):
    count, window = spread.shape
    ahead = window - blk
    for index in range(count // IMG_ROWS):
        picked = slots[:, :IMG_ROWS]
        for image in range(1, slots.shape[1] // IMG_ROWS):
            rows = slots[:, image * IMG_ROWS : (image + 1) * IMG_ROWS]
            picked = jnp.where(starts[TABLE + index] == image, rows, picked)
        slots_here[:, index * IMG_ROWS : (index + 1) * IMG_ROWS] = jnp.broadcast_to(
            picked, (8, IMG_ROWS)
        )
    slot_columns = jnp.broadcast_to(slots_here[0:1, :].astype(jnp.float32), (128, count)).T
    position = starts[8] + lax.broadcasted_iota(jnp.int32, spread.shape, 1)
    match = jnp.where(slot_columns[:, 0:1] == position.astype(jnp.float32), 1.0, 0.0)
    spread[...] = match.astype(jnp.bfloat16)
    hits[...] = jnp.broadcast_to(jnp.max(match, axis=0, keepdims=True), hits.shape)
    line = starts[11]
    parts = []
    for back in range(ahead // blk, -1, -1):
        start = pl.multiple_of(jnp.maximum(line - back, 0) * blk, 128)
        part = docs[:, pl.ds(start, blk)].astype(jnp.float32)
        parts.append(jnp.where(line >= back, part, -1.0))
    doc_row = jnp.concatenate(parts, axis=1)
    doc_columns = jnp.broadcast_to(doc_row, (128, window)).T
    reach = longest + 128
    for block in range(blk // 128):
        first = ahead - longest + block * 128
        key_place = first + lax.broadcasted_iota(jnp.int32, (reach, 128), 0)
        query_place = ahead + block * 128 + lax.broadcasted_iota(jnp.int32, (reach, 128), 1)
        query_docs = doc_row[:, ahead + block * 128 : ahead + block * 128 + 128]
        allowed = (key_place <= query_place) & (doc_columns[first : first + reach] == query_docs)
        bias[block] = jnp.where(allowed, 0.0, -1e30)


def image_rows_kernel(starts, ours, theirs, gain, merged, normed):
    first_side = starts[9] == 0
    mine, other = ours[...], theirs[...]
    merged[...] = jnp.concatenate(
        [jnp.where(first_side, mine, other), jnp.where(first_side, other, mine)], axis=1
    )
    normed[...] = rms_norm(merged[...].astype(jnp.float32), gain[...].reshape(1, -1)).astype(jnp.bfloat16)


def late_kernel(blk, longest, lines, depth, starts, image_rows, spread, hits, bias, *refs):
    sources, near = refs[: 2 * lines], refs[2 * lines + 2 : 4 * lines + 2]
    kept, given = refs[2 * lines : 2 * lines + 2]
    whole, blended, arrived = refs[-3:]
    texts, text_near = sources[0], near[0]
    copies = [pltpu.make_async_copy(texts.at[0], text_near.at[0], arrived.at[0])]
    copies.append(pltpu.make_async_copy(sources[1], near[1], arrived.at[1]))
    for line in range(1, lines):
        for place in (2 * line, 2 * line + 1):
            copies.append(pltpu.make_async_copy(sources[place], near[place], arrived.at[place]))
        copies.append(
            pltpu.make_async_copy(texts.at[line], text_near.at[line], arrived.at[2 * lines + line])
        )
    for copy in copies:
        copy.start()
    ahead = spread.shape[1] - blk
    reach = longest + 128
    factor = math.log2(math.e) / math.sqrt(HD)
    hit = hits[0:1, :] > 0.5
    heads = near[1].shape[0] // (3 * HD)
    if heads * HD < depth:
        blended[...] = jnp.zeros_like(blended)
    for line in range(lines):
        for copy in copies[: 2] if line == 0 else copies[3 * line - 1 : 3 * line + 2]:
            copy.wait()
        if line:
            put_quarters(whole, near[2 * line], near[2 * line + 1], starts, 0)
        weights = whole if line else near[1]
        image_part = lax.dot_general(
            image_rows[...], weights[...], NT, preferred_element_type=jnp.float32
        ).astype(jnp.bfloat16)
        placed = lax.dot_general(
            image_part, spread[...], TN, preferred_element_type=jnp.float32
        )
        for head in range(heads):
            base = head * 3 * HD

            def picked(part, start):
                rows = pl.ds(base + part * HD, HD)
                image = placed[base + part * HD : base + (part + 1) * HD, start:]
                text = text_near[line, rows, start:].astype(jnp.float32)
                return jnp.where(hit[:, start:], image, text)

            queries = (picked(0, ahead) * factor).astype(jnp.bfloat16)
            keys = picked(1, 0).T.astype(jnp.bfloat16)
            values = picked(2, 0).astype(jnp.bfloat16)
            blocks = range(blk // 128)
            firsts = [ahead - longest + block * 128 for block in blocks]
            scores = [
                jnp.dot(
                    keys[first : first + reach],
                    queries[:, block * 128 : block * 128 + 128],
                    preferred_element_type=jnp.float32,
                ) + bias[block]
                for block, first in zip(blocks, firsts)
            ]
            raised = [jnp.exp2(part - jnp.max(part, axis=0, keepdims=True)) for part in scores]
            shares = [1.0 / jnp.sum(part, axis=0, keepdims=True) for part in raised]
            mixed = [
                jnp.dot(
                    values[:, first : first + reach],
                    part.astype(jnp.bfloat16),
                    preferred_element_type=jnp.float32,
                )
                for first, part in zip(firsts, raised)
            ]
            for block in blocks:
                columns = pl.ds(block * 128, 128)
                blended[pl.ds(line * depth + head * HD, HD), columns] = mixed[block] * shares[block]
    attended = blended[...].T.astype(jnp.bfloat16)
    low, high = attended[: blk // 2], attended[blk // 2 :]
    first_side = starts[9] == 0
    kept[...] = jnp.where(first_side, low, high)
    given[...] = jnp.where(first_side, high, low)


def project_kernel(starts, rows, own, *refs):
    quarters, (out, whole) = refs[:4], refs[4:]
    depth = own.shape[0]
    whole[:depth] = own[...]
    size = quarters[0].shape[1]
    for line in range(quarters[0].shape[0]):
        for index in range(4):
            start = pl.multiple_of((line + 1) * depth + starts[4 + index], 16)
            whole[pl.ds(start, size), :] = quarters[index][line]
    total = jnp.dot(rows[...], whole[...], preferred_element_type=jnp.float32)
    out[...] = total.astype(jnp.bfloat16)


def out_kernel(starts, text, slots, merged, kept, out):
    count = text.shape[0]
    position = starts[10] + lax.broadcasted_iota(jnp.int32, (count, merged.shape[0]), 0)
    match = jnp.where(slots[0:1, :] == position, 1.0, 0.0)
    placed = jnp.dot(match.astype(jnp.bfloat16), merged[...], preferred_element_type=jnp.float32)
    hit = jnp.max(match, axis=1, keepdims=True) > 0.5
    embedded = jnp.where(hit, placed, text[...].astype(jnp.float32))
    out[...] = embedded + kept[...].astype(jnp.float32)


SMEM = pl.BlockSpec(memory_space=pltpu.SMEM)


def kernel_call(body, name, results, *operands, scratch=(), grid=(), specs={}, out_specs=None, aliases={}, room=56):
    return pl.pallas_call(
        body,
        grid=grid,
        in_specs=[SMEM]
        + [
            specs.get(place, whole_block(value.shape))
            for place, value in enumerate(operands)
            if place
        ],
        out_specs=out_specs or [whole_block(shape) for shape, _ in results],
        out_shape=[jax.ShapeDtypeStruct(shape, dtype) for shape, dtype in results],
        scratch_shapes=list(scratch),
        input_output_aliases=aliases,
        compiler_params=pltpu.CompilerParams(vmem_limit_bytes=room << 20),
        cost_estimate=pl.CostEstimate(flops=1, bytes_accessed=1, transcendentals=0),
        name=name,
    )(*operands)


def quarters_spec(values, line_of):
    shape = (2, 1) + values.shape[2:]
    return pl.BlockSpec(shape, lambda k: (0, line_of(k), 0, 0))


def project(starts, rows, own, quarters):
    lines = quarters[0].shape[0] + 1
    return kernel_call(
        project_kernel, "project", [((rows.shape[0], own.shape[1]), jnp.bfloat16)],
        starts, rows, own, *quarters,
        scratch=[pltpu.VMEM((lines * own.shape[0], own.shape[1]), jnp.bfloat16)],
    )


def mlp_kernel(mine, other, gain, w_in, w_back, out_mine, out_other, rows, total):
    step = pl.program_id(0)
    count = mine.shape[0]

    @pl.when(step == 0)
    def _():
        for place, part in ((0, mine), (count, other)):
            normed = layer_norm(part[...].astype(jnp.float32), gain[...].reshape(1, -1))
            rows[pl.ds(place, count), :] = normed.astype(jnp.bfloat16)
        total[...] = jnp.zeros_like(total)

    wide = jnp.dot(rows[...], w_in[...], preferred_element_type=jnp.float32)
    hidden = 0.5 * wide * (1.0 + lax.erf(wide * math.sqrt(0.5)))
    total[...] += jnp.dot(
        hidden.astype(jnp.bfloat16), w_back[...], preferred_element_type=jnp.float32
    )

    @pl.when(step == pl.num_programs(0) - 1)
    def _():
        out_mine[...] = total[:count].astype(jnp.bfloat16)
        out_other[...] = total[count:].astype(jnp.bfloat16)


def whole_block(shape):
    return pl.BlockSpec(shape, lambda *_: (0,) * len(shape))


def mlp(mine, other, gain, w_in, w_back):
    count, width = mine.shape
    units = w_in.shape[1]
    step = 256
    return pl.pallas_call(
        mlp_kernel,
        grid=(units // step,),
        in_specs=[
            whole_block((count, width)),
            whole_block((count, width)),
            whole_block((width,)),
            pl.BlockSpec((width, step), lambda i: (0, i)),
            pl.BlockSpec((step, width), lambda i: (i, 0)),
        ],
        out_specs=[whole_block((count, width))] * 2,
        out_shape=[jax.ShapeDtypeStruct((count, width), jnp.bfloat16)] * 2,
        scratch_shapes=[
            pltpu.VMEM((2 * count, width), jnp.bfloat16),
            pltpu.VMEM((2 * count, width), jnp.float32),
        ],
        compiler_params=pltpu.CompilerParams(vmem_limit_bytes=16 << 20),
        cost_estimate=pl.CostEstimate(flops=1, bytes_accessed=1, transcendentals=0),
        name="mlp_rows",
    )(mine, other, gain, w_in, w_back)


def spread_kernel(lines, place, rows, *refs):
    parts, (gain, kept, given) = refs[:-3], refs[-3:]
    wide = rows[...].astype(jnp.float32)
    for part in parts:
        wide = wide + part[...].astype(jnp.float32)
    normed = layer_norm(wide, gain[...].reshape(1, -1)).astype(jnp.bfloat16)
    size = kept.shape[2]
    quads = kept.shape[1]
    to = lax.broadcasted_iota(jnp.int32, (4 * quads, 4 * quads), 0)
    by = lax.broadcasted_iota(jnp.int32, (4 * quads, 4 * quads), 1)
    moves = jnp.where(by == to % quads * 4 + to // quads, 1.0, 0.0).astype(jnp.bfloat16)
    sorted_rows = jnp.dot(moves, normed, preferred_element_type=jnp.float32).astype(jnp.bfloat16)
    first_side = place[9] == 0
    for target in range(lines):
        row, base = target // (lines // 4), target % (lines // 4) * 2 * size
        picked = sorted_rows[row * quads : (row + 1) * quads]
        low, high = picked[:, base : base + size], picked[:, base + size : base + 2 * size]
        turn = lax.rem(target + lines - place[11], lines)
        kept[turn] = jnp.where(first_side, low, high)
        given[turn] = jnp.where(first_side, high, low)


def spread_rows(place, rows, parts, gain, lines):
    count, width = rows.shape
    shape = (lines, count // 4, 2 * width // lines)
    return pl.pallas_call(
        functools.partial(spread_kernel, lines),
        in_specs=[pl.BlockSpec(memory_space=pltpu.SMEM)]
        + [whole_block((count, width))] * (1 + len(parts))
        + [whole_block((width,))],
        out_specs=[whole_block(shape)] * 2,
        out_shape=[jax.ShapeDtypeStruct(shape, jnp.bfloat16)] * 2,
        compiler_params=pltpu.CompilerParams(vmem_limit_bytes=56 << 20),
        cost_estimate=pl.CostEstimate(flops=1, bytes_accessed=1, transcendentals=0),
        name="spread_rows",
    )(place, rows, *parts, gain)


def merge_kernel(place, *refs):
    blocks, (weights, kept, given, rows) = refs[:-4], refs[-4:]
    lines = len(blocks)
    quads = blocks[0].shape[0] // 2
    for index, block in enumerate(blocks):
        base = lax.rem(place[11] + lines - index, lines) * 2
        for half in (0, 1):
            start = (base + (place[9] if half == 0 else 1 - place[9])) * quads
            rows[pl.ds(pl.multiple_of(start, 16), quads), :] = block[half * quads : half * quads + quads]
    wide = jnp.dot(rows[...], weights[...], preferred_element_type=jnp.float32)
    half = kept.shape[1]
    low, high = wide[:, :half], wide[:, half:]
    first_side = place[9] == 0
    kept[...] = jnp.where(first_side, low, high)
    given[...] = jnp.where(first_side, high, low).astype(jnp.bfloat16)


def split_kernel(needed, place, kept, got, *outs):
    for index, out in enumerate(outs):
        for image in range(needed):
            rows = pl.ds(pl.multiple_of(place[TABLE + index * needed + image] * IMG_ROWS, 16), IMG_ROWS)
            both = kept[rows, :] + got[rows, :].astype(jnp.float32)
            out[image * IMG_ROWS : (image + 1) * IMG_ROWS] = both.astype(jnp.bfloat16)


def merge(place, blocks, weights):
    count, size = blocks[0].shape
    rows, half = count * len(blocks), weights.shape[1] // 2
    return pl.pallas_call(
        merge_kernel,
        in_specs=[pl.BlockSpec(memory_space=pltpu.SMEM)]
        + [whole_block((count, size))] * len(blocks)
        + [whole_block(weights.shape)],
        out_specs=[whole_block((rows, half))] * 2,
        out_shape=[
            jax.ShapeDtypeStruct((rows, half), jnp.float32),
            jax.ShapeDtypeStruct((rows, half), jnp.bfloat16),
        ],
        scratch_shapes=[pltpu.VMEM((rows, size), jnp.bfloat16)],
        compiler_params=pltpu.CompilerParams(vmem_limit_bytes=16 << 20),
        cost_estimate=pl.CostEstimate(flops=1, bytes_accessed=1, transcendentals=0),
        name="merge_rows",
    )(place, *blocks, weights)


def after(values, first):
    return lax.optimization_barrier((values, first))[0]


class Queue:
    def __init__(self):
        self.last = []

    def held(self, value):
        return after(value, self.last) if self.last else value

    def passed(self, value):
        self.last = [value]
        return value

    def wait(self, value):
        self.last = self.last + [value]
        return value


def quarter_size(rows):
    return -(-rows // 64) * 16


def quarter_start(rows, index):
    return jnp.minimum(index * quarter_size(rows), rows - quarter_size(rows))


def padded(weights):
    return jnp.pad(weights, ((0, -weights.shape[0] % 16), (0, 0)))


def own_quarter(weights):
    place = lax.axis_index("req") % 4
    size = quarter_size(weights.shape[0])
    return lax.dynamic_slice_in_dim(weights, quarter_start(weights.shape[0], place), size, 0)


def other_copy(values, flip):
    return lax.ppermute(values, "req", [(i, i ^ flip) for i in range(lax.axis_size("req"))])


def line_neighbours(values, tp_size):
    lines = tp_size // 2
    if lines != 4:
        return [turned(values, tp_size, k) for k in range(1, lines)]
    up = lax.ppermute(values, "tp", [(i, i + 2) for i in range(tp_size - 2)])
    down = lax.ppermute(values, "tp", [(i + 2, i) for i in range(tp_size - 2)])
    return [up, turned(values, tp_size, 2), down]


def line_ends(parts, tp_size, queue):
    if tp_size // 2 != 4:
        return parts
    line = lax.axis_index("tp") // 2
    ends = lax.ppermute(queue.held(parts[1]), "tp", [(2, 0), (3, 1), (4, 6), (5, 7)])
    return [jnp.where(line == 0, ends, parts[0]), parts[1], jnp.where(line == 3, ends, parts[2])]


def shards(
    patches, vis_gain, w_fc1, w_fc2, merge_gain, w_merge, slots, text, docs, dec_gain, w_qkv, w_out
):
    patch_rows = patches[0]
    text_rows = text[0]
    width = patch_rows.shape[1]
    seq_here = text_rows.shape[0]
    tp_size = lax.axis_size("tp")
    lines = tp_size // 2
    line = lax.axis_index("tp") // 2
    side = lax.axis_index("tp") % 2

    blk = 2 * seq_here
    longest = seq_here * tp_size // 4
    halo = -(-longest // blk)
    ahead = halo * blk
    window = ahead + blk
    qkv_own = padded(w_qkv.T)
    out_own = padded(w_out)
    columns, depth = qkv_own.shape[0], out_own.shape[0]
    place = lax.axis_index("req") % 4
    starts = jnp.stack(
        [quarter_start(columns, place ^ i) for i in (0, 1, 2, 3)]
        + [quarter_start(depth, place ^ i) for i in (0, 1, 2, 3)]
        + [line * blk - ahead, side, (2 * line + side) * seq_here, line]
    ).astype(jnp.int32)
    bf16 = jnp.bfloat16

    images = slots.shape[1] // IMG_ROWS
    span = seq_here * tp_size // images
    tables = []
    for target in range(lines):
        held = []
        for place_of in range(images):
            low = place_of * span if place_of < images - 1 else images * span - IMG_ROWS
            inside = low < (target + 1) * blk and (place_of + 1) * span > target * blk - ahead
            held.append((not inside, (place_of - images // 2) % images))
        tables.append(sorted(held))
    needed = max(sum(not outside for outside, _ in held) for held in tables)
    table = jnp.array([[image for _, image in held[:needed]] for held in tables], jnp.int32)
    turned_table = table[(line + jnp.arange(lines)) % lines]
    starts = jnp.concatenate([starts, turned_table.reshape(-1)])
    count = needed * IMG_ROWS
    queue = Queue()
    rounds = [k for k in range(1, lines) if k != lines // 2]
    middle = lines // 2
    other, sums, part = {}, {}, {}

    def run_mlp(k, mine):
        own, given = mlp(queue.held(mine), other[k], vis_gain, w_fc1, w_fc2)
        queue.passed((own, given))
        part[k] = own
        return swap_pair(given, tp_size)

    def add_pair(k, got):
        pair = (queue.held(part[k]).astype(jnp.float32) + got.astype(jnp.float32)).astype(bf16)
        queue.passed(pair)
        return turned(pair, tp_size, lines - k)

    swapping = swap_pair(patch_rows, tp_size)
    moving = {k: turned(patch_rows, tp_size, k) for k in rounds + [middle]}
    text_other = swap_pair(text_rows, tp_size)
    qkv_quarter, out_quarter = queue.passed((own_quarter(qkv_own), own_quarter(out_own)))
    other[0] = queue.wait(swapping)
    mine, swapping = {}, {}
    for k in rounds + [middle]:
        mine[k] = queue.wait(moving[k])
    text_other = queue.wait(text_other)
    for k in rounds + [middle]:
        swapping[k] = swap_pair(queue.held(mine[k]), tp_size)
    qkv_moving, qkv_ours, qkv_theirs = {}, {}, {}
    place_of = {0: 0, middle: lines - 1, **{k: i + 1 for i, k in enumerate(rounds)}}

    def move_weights(k, part=0, parts=1):
        size = qkv_quarter.shape[0] // parts
        piece = qkv_quarter[part * size : (part + 1) * size]
        qkv_moving.setdefault(k, []).append(turned(queue.held(piece), tp_size, k))

    def cross_weights(k):
        halves = queue.wait(qkv_moving[k])
        qkv_moving[k] = halves[0] if len(halves) == 1 else jnp.concatenate(queue.held(halves))
        qkv_theirs[k] = other_copy(queue.held(qkv_moving[k]), 2)

    def share_weights(k):
        both = jnp.stack([queue.held(qkv_moving[k]), queue.wait(qkv_theirs[k])])
        qkv_ours[k] = queue.passed(both[:, None])
        qkv_theirs[k] = other_copy(qkv_ours[k], 1)

    text_back = []
    for steps_back in range(1, halo + 1):
        steps = [(i, i + 2 * steps_back) for i in range(tp_size - 2 * steps_back)]
        text_back.append(lax.ppermute(queue.held(text_rows), "tp", steps))
    back = {0: run_mlp(0, patch_rows)}
    for index, k in enumerate(rounds):
        other[k] = queue.wait(swapping[k])
        if index == 1:
            text_back = queue.wait(text_back)
            move_weights(middle, 0, 2)
        back[k] = run_mlp(k, mine[k])
    other[middle] = queue.wait(swapping[middle])
    back[middle] = run_mlp(middle, mine[middle])
    queue.wait(qkv_moving[middle][0])
    for k in rounds:
        sums[k] = add_pair(k, queue.wait(back[k]))
    got = queue.wait(back[middle])
    for k in rounds:
        queue.wait(sums[k])
    sums[middle] = add_pair(middle, got)
    move_weights(middle, 1, 2)
    pieces = []
    for rows in text_back[::-1]:
        pieces += [rows, swap_pair(queue.held(rows), tp_size)]
    spread, hits, bias, slots_here = queue.passed(kernel_call(
        functools.partial(mask_kernel, blk, longest), "masks",
        [
            ((count, window), bf16),
            ((8, window), jnp.float32),
            ((blk // 128, longest + 128, 128), jnp.float32),
            ((8, count), jnp.int32),
        ],
        starts, queue.held(slots), docs,
    ))
    sums[0] = part[0]
    sums = [queue.wait(back[0])] + [queue.wait(sums[k]) for k in range(lines)]
    cross_weights(middle)
    kept, given = queue.passed(
        spread_rows(starts, queue.held(patch_rows), sums, merge_gain, lines)
    )
    got = swap_pair(queue.held(given), tp_size)
    move_weights(rounds[0])
    pieces = queue.wait(pieces) + [text_rows, text_other]
    text_normed, text_parts = queue.passed(kernel_call(
        text_kernel, "text_first", [((window, width), bf16), ((lines, columns, window), bf16)],
        starts, queue.held(dec_gain), qkv_own, *pieces,
        grid=(1,),
        out_specs=[
            whole_block((window, width)),
            pl.BlockSpec((1, columns, window), lambda _: (0, 0, 0)),
        ],
    ))

    def run_text(text_parts, k):
        return queue.passed(kernel_call(
            text_next_kernel, "text_next", [((lines, columns, window), bf16)],
            starts, queue.held(text_normed), qkv_ours[k], queue.wait(qkv_theirs[k]), text_parts,
            grid=(window // 256,),
            specs={
                1: pl.BlockSpec((256, width), lambda i: (i, 0)),
                4: pl.BlockSpec(memory_space=pl.ANY),
            },
            out_specs=[pl.BlockSpec((1, columns, 256), lambda i: (place_of[k], 0, i))],
            scratch=[pltpu.VMEM((columns, width), bf16)],
            aliases={4: 0},
        ))[0]

    got = queue.wait(got)
    cross_weights(rounds[0])
    share_weights(middle)
    blocks = queue.passed([jnp.concatenate([queue.held(kept[k]), got[k]]) for k in range(lines)])
    blocks = [blocks[0]] + [turned(blocks[k], tp_size, k) for k in range(1, lines)]
    queue.wait(blocks)
    kept, given = queue.passed(merge(starts, [queue.held(blocks[0])] + blocks[1:], w_merge))
    half = kept.shape[1]
    got = swap_pair(given, tp_size)
    for k in rounds[1:]:
        move_weights(k)
    text_parts = run_text(text_parts, middle)
    got = queue.wait(got)
    share = queue.passed(kernel_call(
        functools.partial(split_kernel, needed), "image_shares", [((count, half), bf16)] * lines,
        starts, queue.held(kept), got,
    ))
    moving = [turned(share[k], tp_size, k) for k in range(1, lines)]
    for k in rounds[1:]:
        cross_weights(k)
    share_weights(rounds[0])
    text_parts = run_text(text_parts, rounds[0])
    total = queue.held(share[0]).astype(jnp.float32)
    for block in queue.wait(moving):
        total = total + block.astype(jnp.float32)
    total = queue.passed(total.astype(bf16))
    for k in rounds[1:]:
        share_weights(k)
    far = swap_pair(queue.held(total), tp_size)
    out_moving = [turned(queue.held(out_quarter), tp_size, k) for k in rounds + [middle]]
    for k in rounds[1:]:
        text_parts = run_text(text_parts, k)
    merged, image_rows = queue.passed(kernel_call(
        image_rows_kernel, "image_rows", [((count, width), bf16)] * 2,
        starts, queue.held(total), queue.wait(far), dec_gain,
    ))
    line_pieces = [x[k] for k in rounds + [middle] for x in (qkv_ours, qkv_theirs)]
    sources = [text_parts, qkv_own] + line_pieces
    out_near = queue.passed(jnp.stack(queue.wait([queue.held(part) for part in out_moving])))
    out_far = other_copy(out_near, 2)
    out_beside = other_copy(out_near, 1)
    kept, given = queue.passed(kernel_call(
        functools.partial(late_kernel, blk, longest, lines, depth), "late_attention",
        [((seq_here, lines * depth), bf16)] * 2,
        starts, queue.held(image_rows), spread, hits, bias, *sources,
        specs={5 + i: pl.BlockSpec(memory_space=pl.ANY) for i in range(2 * lines)},
        scratch=[pltpu.VMEM(source.shape, bf16) for source in sources] + [
            pltpu.VMEM((columns, width), bf16),
            pltpu.VMEM((lines * depth, blk), jnp.float32),
            pltpu.SemaphoreType.DMA((3 * lines,)),
        ],
        room=32,
    ))
    out_far = queue.wait(out_far)
    out_across = other_copy(queue.held(out_far), 1)
    quarters = [out_near, queue.wait(out_beside), out_far, queue.wait(out_across)]
    (given,) = queue.passed(project(starts, queue.held(given), out_own, quarters))
    got = swap_pair(given, tp_size)
    (kept,) = queue.passed(project(starts, queue.held(kept), out_own, quarters))
    (own_rows,) = queue.passed(kernel_call(
        out_kernel, "out_rows", [((seq_here, width), jnp.float32)],
        starts, queue.held(text_rows), slots_here, merged, kept,
    ))
    decoded = (queue.held(own_rows) + queue.wait(got).astype(jnp.float32)).astype(bf16)
    return decoded[None]


def solution(mesh):
    placed = (
        P("req", "tp", None),
        P(),
        P(None, "tp"),
        P("tp", None),
        P(),
        P("tp", None),
        P("req", None),
        P("req", "tp", None),
        P("req", None),
        P(),
        P(None, "tp"),
        P("tp", None),
    )
    return jax.shard_map(
        shards, mesh=mesh, in_specs=placed, out_specs=P("req", "tp", None), check_vma=False
    )
```

```python
import functools
import math

import jax
import jax.numpy as jnp
from jax import lax
from jax.experimental import pallas as pl
from jax.experimental.pallas import tpu as pltpu
from jax.sharding import PartitionSpec as P

HD = 104
IMG_ROWS = 64
TABLE = 12


EPSILON = 1e-06


def layer_norm(values, gains):
    average = jnp.mean(values, axis=-1, keepdims=True)
    centred = values - average
    variance = jnp.mean(centred * centred, axis=-1, keepdims=True)
    return centred * lax.rsqrt(variance + EPSILON) * gains


def rms_norm(values, gains):
    return values * lax.rsqrt(jnp.mean(values * values, axis=-1, keepdims=True) + EPSILON) * gains


def pair_steps(tp_size):
    return [(i, i ^ 1) for i in range(tp_size)]


def turn_steps(tp_size, turn):
    lines = tp_size // 2
    return [(a * 2 + b, ((a + turn) % lines) * 2 + b) for a in range(lines) for b in range(2)]


def swap_pair(values, tp_size):
    return lax.ppermute(values, "tp", pair_steps(tp_size))


def turned(values, tp_size, turn):
    return lax.ppermute(values, "tp", turn_steps(tp_size, turn))


NT = (((1,), (1,)), ((), ()))
TN = (((0,), (0,)), ((), ()))


def put_quarters(whole, ours, theirs, starts, offset):
    size = ours.shape[2]
    for index in range(4):
        quarter = ours[index // 2, 0] if index % 2 == 0 else theirs[index // 2, 0]
        start = pl.multiple_of(starts[offset + index], 16)
        whole[pl.ds(start, size), :] = quarter


def text_kernel(starts, gain, own, *refs):
    pieces, (rows, out) = refs[:-2], refs[-2:]
    count = pieces[0].shape[0]
    first_side = starts[9] == 0
    for index in range(0, len(pieces), 2):
        mine, other = pieces[index][...], pieces[index + 1][...]
        both = (jnp.where(first_side, mine, other), jnp.where(first_side, other, mine))
        for half, part in enumerate(both):
            normed = rms_norm(part.astype(jnp.float32), gain[...].reshape(1, -1))
            rows[pl.ds((index + half) * count, count), :] = normed.astype(jnp.bfloat16)
    out[0] = lax.dot_general(
        own[...], rows[...], NT, preferred_element_type=jnp.float32
    ).astype(jnp.bfloat16)


def text_next_kernel(starts, rows, ours, theirs, before, out, whole):
    @pl.when(pl.program_id(0) == 0)
    def _():
        put_quarters(whole, ours, theirs, starts, 0)

    out[0] = lax.dot_general(
        whole[...], rows[...], NT, preferred_element_type=jnp.float32
    ).astype(jnp.bfloat16)


def mask_kernel(blk, longest, starts, slots, docs, spread, hits, bias, slots_here):
    count, window = spread.shape
    ahead = window - blk
    for index in range(count // IMG_ROWS):
        picked = slots[:, :IMG_ROWS]
        for image in range(1, slots.shape[1] // IMG_ROWS):
            rows = slots[:, image * IMG_ROWS : (image + 1) * IMG_ROWS]
            picked = jnp.where(starts[TABLE + index] == image, rows, picked)
        slots_here[:, index * IMG_ROWS : (index + 1) * IMG_ROWS] = jnp.broadcast_to(
            picked, (8, IMG_ROWS)
        )
    slot_columns = jnp.broadcast_to(slots_here[0:1, :].astype(jnp.float32), (128, count)).T
    position = starts[8] + lax.broadcasted_iota(jnp.int32, spread.shape, 1)
    match = jnp.where(slot_columns[:, 0:1] == position.astype(jnp.float32), 1.0, 0.0)
    spread[...] = match.astype(jnp.bfloat16)
    hits[...] = jnp.broadcast_to(jnp.max(match, axis=0, keepdims=True), hits.shape)
    line = starts[11]
    parts = []
    for back in range(ahead // blk, -1, -1):
        start = pl.multiple_of(jnp.maximum(line - back, 0) * blk, 128)
        part = docs[:, pl.ds(start, blk)].astype(jnp.float32)
        parts.append(jnp.where(line >= back, part, -1.0))
    doc_row = jnp.concatenate(parts, axis=1)
    doc_columns = jnp.broadcast_to(doc_row, (128, window)).T
    reach = longest + 128
    for block in range(blk // 128):
        first = ahead - longest + block * 128
        key_place = first + lax.broadcasted_iota(jnp.int32, (reach, 128), 0)
        query_place = ahead + block * 128 + lax.broadcasted_iota(jnp.int32, (reach, 128), 1)
        query_docs = doc_row[:, ahead + block * 128 : ahead + block * 128 + 128]
        allowed = (key_place <= query_place) & (doc_columns[first : first + reach] == query_docs)
        bias[block] = jnp.where(allowed, 0.0, -1e30)


def image_rows_kernel(starts, ours, theirs, gain, merged, normed):
    first_side = starts[9] == 0
    mine, other = ours[...], theirs[...]
    merged[...] = jnp.concatenate(
        [jnp.where(first_side, mine, other), jnp.where(first_side, other, mine)], axis=1
    )
    normed[...] = rms_norm(merged[...].astype(jnp.float32), gain[...].reshape(1, -1)).astype(jnp.bfloat16)


def late_kernel(blk, longest, lines, depth, starts, image_rows, spread, hits, bias, *refs):
    sources, near = refs[: 2 * lines], refs[2 * lines + 2 : 4 * lines + 2]
    kept, given = refs[2 * lines : 2 * lines + 2]
    whole, blended, arrived = refs[-3:]
    texts, text_near = sources[0], near[0]
    copies = [pltpu.make_async_copy(texts.at[0], text_near.at[0], arrived.at[0])]
    copies.append(pltpu.make_async_copy(sources[1], near[1], arrived.at[1]))
    for line in range(1, lines):
        for place in (2 * line, 2 * line + 1):
            copies.append(pltpu.make_async_copy(sources[place], near[place], arrived.at[place]))
        copies.append(
            pltpu.make_async_copy(texts.at[line], text_near.at[line], arrived.at[2 * lines + line])
        )
    for copy in copies:
        copy.start()
    ahead = spread.shape[1] - blk
    reach = longest + 128
    factor = math.log2(math.e) / math.sqrt(HD)
    hit = hits[0:1, :] > 0.5
    heads = near[1].shape[0] // (3 * HD)
    if heads * HD < depth:
        blended[...] = jnp.zeros_like(blended)
    for line in range(lines):
        for copy in copies[: 2] if line == 0 else copies[3 * line - 1 : 3 * line + 2]:
            copy.wait()
        if line:
            put_quarters(whole, near[2 * line], near[2 * line + 1], starts, 0)
        weights = whole if line else near[1]
        image_part = lax.dot_general(
            image_rows[...], weights[...], NT, preferred_element_type=jnp.float32
        ).astype(jnp.bfloat16)
        placed = lax.dot_general(
            image_part, spread[...], TN, preferred_element_type=jnp.float32
        )
        for head in range(heads):
            base = head * 3 * HD

            def picked(part, start):
                rows = pl.ds(base + part * HD, HD)
                image = placed[base + part * HD : base + (part + 1) * HD, start:]
                text = text_near[line, rows, start:].astype(jnp.float32)
                return jnp.where(hit[:, start:], image, text)

            queries = (picked(0, ahead) * factor).astype(jnp.bfloat16)
            keys = picked(1, 0).T.astype(jnp.bfloat16)
            values = picked(2, 0).astype(jnp.bfloat16)
            blocks = range(blk // 128)
            firsts = [ahead - longest + block * 128 for block in blocks]
            scores = [
                jnp.dot(
                    keys[first : first + reach],
                    queries[:, block * 128 : block * 128 + 128],
                    preferred_element_type=jnp.float32,
                ) + bias[block]
                for block, first in zip(blocks, firsts)
            ]
            raised = [jnp.exp2(part - jnp.max(part, axis=0, keepdims=True)) for part in scores]
            shares = [1.0 / jnp.sum(part, axis=0, keepdims=True) for part in raised]
            mixed = [
                jnp.dot(
                    values[:, first : first + reach],
                    part.astype(jnp.bfloat16),
                    preferred_element_type=jnp.float32,
                )
                for first, part in zip(firsts, raised)
            ]
            for block in blocks:
                columns = pl.ds(block * 128, 128)
                blended[pl.ds(line * depth + head * HD, HD), columns] = mixed[block] * shares[block]
    attended = blended[...].T.astype(jnp.bfloat16)
    low, high = attended[: blk // 2], attended[blk // 2 :]
    first_side = starts[9] == 0
    kept[...] = jnp.where(first_side, low, high)
    given[...] = jnp.where(first_side, high, low)


def project_kernel(starts, rows, own, *refs):
    quarters, (out, whole) = refs[:4], refs[4:]
    depth = own.shape[0]
    whole[:depth] = own[...]
    size = quarters[0].shape[1]
    for line in range(quarters[0].shape[0]):
        for index in range(4):
            start = pl.multiple_of((line + 1) * depth + starts[4 + index], 16)
            whole[pl.ds(start, size), :] = quarters[index][line]
    total = jnp.dot(rows[...], whole[...], preferred_element_type=jnp.float32)
    out[...] = total.astype(jnp.bfloat16)


def out_kernel(starts, text, slots, merged, kept, out):
    count = text.shape[0]
    position = starts[10] + lax.broadcasted_iota(jnp.int32, (count, merged.shape[0]), 0)
    match = jnp.where(slots[0:1, :] == position, 1.0, 0.0)
    placed = jnp.dot(match.astype(jnp.bfloat16), merged[...], preferred_element_type=jnp.float32)
    hit = jnp.max(match, axis=1, keepdims=True) > 0.5
    embedded = jnp.where(hit, placed, text[...].astype(jnp.float32))
    out[...] = embedded + kept[...].astype(jnp.float32)


SMEM = pl.BlockSpec(memory_space=pltpu.SMEM)


def kernel_call(body, name, results, *operands, scratch=(), grid=(), specs={}, out_specs=None, aliases={}, room=56):
    return pl.pallas_call(
        body,
        grid=grid,
        in_specs=[SMEM]
        + [
            specs.get(place, whole_block(value.shape))
            for place, value in enumerate(operands)
            if place
        ],
        out_specs=out_specs or [whole_block(shape) for shape, _ in results],
        out_shape=[jax.ShapeDtypeStruct(shape, dtype) for shape, dtype in results],
        scratch_shapes=list(scratch),
        input_output_aliases=aliases,
        compiler_params=pltpu.CompilerParams(vmem_limit_bytes=room << 20),
        cost_estimate=pl.CostEstimate(flops=1, bytes_accessed=1, transcendentals=0),
        name=name,
    )(*operands)


def quarters_spec(values, line_of):
    shape = (2, 1) + values.shape[2:]
    return pl.BlockSpec(shape, lambda k: (0, line_of(k), 0, 0))


def project(starts, rows, own, quarters):
    lines = quarters[0].shape[0] + 1
    return kernel_call(
        project_kernel, "project", [((rows.shape[0], own.shape[1]), jnp.bfloat16)],
        starts, rows, own, *quarters,
        scratch=[pltpu.VMEM((lines * own.shape[0], own.shape[1]), jnp.bfloat16)],
    )


def mlp_kernel(mine, other, gain, w_in, w_back, out_mine, out_other, rows, total):
    step = pl.program_id(0)
    count = mine.shape[0]

    @pl.when(step == 0)
    def _():
        for place, part in ((0, mine), (count, other)):
            normed = layer_norm(part[...].astype(jnp.float32), gain[...].reshape(1, -1))
            rows[pl.ds(place, count), :] = normed.astype(jnp.bfloat16)
        total[...] = jnp.zeros_like(total)

    wide = jnp.dot(rows[...], w_in[...], preferred_element_type=jnp.float32)
    hidden = 0.5 * wide * (1.0 + lax.erf(wide * math.sqrt(0.5)))
    total[...] += jnp.dot(
        hidden.astype(jnp.bfloat16), w_back[...], preferred_element_type=jnp.float32
    )

    @pl.when(step == pl.num_programs(0) - 1)
    def _():
        out_mine[...] = total[:count].astype(jnp.bfloat16)
        out_other[...] = total[count:].astype(jnp.bfloat16)


def whole_block(shape):
    return pl.BlockSpec(shape, lambda *_: (0,) * len(shape))


def mlp(mine, other, gain, w_in, w_back):
    count, width = mine.shape
    units = w_in.shape[1]
    step = 256
    return pl.pallas_call(
        mlp_kernel,
        grid=(units // step,),
        in_specs=[
            whole_block((count, width)),
            whole_block((count, width)),
            whole_block((width,)),
            pl.BlockSpec((width, step), lambda i: (0, i)),
            pl.BlockSpec((step, width), lambda i: (i, 0)),
        ],
        out_specs=[whole_block((count, width))] * 2,
        out_shape=[jax.ShapeDtypeStruct((count, width), jnp.bfloat16)] * 2,
        scratch_shapes=[
            pltpu.VMEM((2 * count, width), jnp.bfloat16),
            pltpu.VMEM((2 * count, width), jnp.float32),
        ],
        compiler_params=pltpu.CompilerParams(vmem_limit_bytes=16 << 20),
        cost_estimate=pl.CostEstimate(flops=1, bytes_accessed=1, transcendentals=0),
        name="mlp_rows",
    )(mine, other, gain, w_in, w_back)


def spread_kernel(lines, place, rows, *refs):
    parts, (gain, kept, given) = refs[:-3], refs[-3:]
    wide = rows[...].astype(jnp.float32)
    for part in parts:
        wide = wide + part[...].astype(jnp.float32)
    normed = layer_norm(wide, gain[...].reshape(1, -1)).astype(jnp.bfloat16)
    size = kept.shape[2]
    quads = kept.shape[1]
    to = lax.broadcasted_iota(jnp.int32, (4 * quads, 4 * quads), 0)
    by = lax.broadcasted_iota(jnp.int32, (4 * quads, 4 * quads), 1)
    moves = jnp.where(by == to % quads * 4 + to // quads, 1.0, 0.0).astype(jnp.bfloat16)
    sorted_rows = jnp.dot(moves, normed, preferred_element_type=jnp.float32).astype(jnp.bfloat16)
    first_side = place[9] == 0
    for target in range(lines):
        row, base = target // (lines // 4), target % (lines // 4) * 2 * size
        picked = sorted_rows[row * quads : (row + 1) * quads]
        low, high = picked[:, base : base + size], picked[:, base + size : base + 2 * size]
        turn = lax.rem(target + lines - place[11], lines)
        kept[turn] = jnp.where(first_side, low, high)
        given[turn] = jnp.where(first_side, high, low)


def spread_rows(place, rows, parts, gain, lines):
    count, width = rows.shape
    shape = (lines, count // 4, 2 * width // lines)
    return pl.pallas_call(
        functools.partial(spread_kernel, lines),
        in_specs=[pl.BlockSpec(memory_space=pltpu.SMEM)]
        + [whole_block((count, width))] * (1 + len(parts))
        + [whole_block((width,))],
        out_specs=[whole_block(shape)] * 2,
        out_shape=[jax.ShapeDtypeStruct(shape, jnp.bfloat16)] * 2,
        compiler_params=pltpu.CompilerParams(vmem_limit_bytes=56 << 20),
        cost_estimate=pl.CostEstimate(flops=1, bytes_accessed=1, transcendentals=0),
        name="spread_rows",
    )(place, rows, *parts, gain)


def merge_kernel(place, *refs):
    blocks, (weights, kept, given, rows) = refs[:-4], refs[-4:]
    lines = len(blocks)
    quads = blocks[0].shape[0] // 2
    for index, block in enumerate(blocks):
        base = lax.rem(place[11] + lines - index, lines) * 2
        for half in (0, 1):
            start = (base + (place[9] if half == 0 else 1 - place[9])) * quads
            rows[pl.ds(pl.multiple_of(start, 16), quads), :] = block[half * quads : half * quads + quads]
    wide = jnp.dot(rows[...], weights[...], preferred_element_type=jnp.float32)
    half = kept.shape[1]
    low, high = wide[:, :half], wide[:, half:]
    first_side = place[9] == 0
    kept[...] = jnp.where(first_side, low, high)
    given[...] = jnp.where(first_side, high, low).astype(jnp.bfloat16)


def split_kernel(needed, place, kept, got, *outs):
    for index, out in enumerate(outs):
        for image in range(needed):
            rows = pl.ds(pl.multiple_of(place[TABLE + index * needed + image] * IMG_ROWS, 16), IMG_ROWS)
            both = kept[rows, :] + got[rows, :].astype(jnp.float32)
            out[image * IMG_ROWS : (image + 1) * IMG_ROWS] = both.astype(jnp.bfloat16)


def merge(place, blocks, weights):
    count, size = blocks[0].shape
    rows, half = count * len(blocks), weights.shape[1] // 2
    return pl.pallas_call(
        merge_kernel,
        in_specs=[pl.BlockSpec(memory_space=pltpu.SMEM)]
        + [whole_block((count, size))] * len(blocks)
        + [whole_block(weights.shape)],
        out_specs=[whole_block((rows, half))] * 2,
        out_shape=[
            jax.ShapeDtypeStruct((rows, half), jnp.float32),
            jax.ShapeDtypeStruct((rows, half), jnp.bfloat16),
        ],
        scratch_shapes=[pltpu.VMEM((rows, size), jnp.bfloat16)],
        compiler_params=pltpu.CompilerParams(vmem_limit_bytes=16 << 20),
        cost_estimate=pl.CostEstimate(flops=1, bytes_accessed=1, transcendentals=0),
        name="merge_rows",
    )(place, *blocks, weights)


def after(values, first):
    return lax.optimization_barrier((values, first))[0]


class Queue:
    def __init__(self):
        self.last = []

    def held(self, value):
        return after(value, self.last) if self.last else value

    def passed(self, value):
        self.last = [value]
        return value

    def wait(self, value):
        self.last = self.last + [value]
        return value


def quarter_size(rows):
    return -(-rows // 64) * 16


def quarter_start(rows, index):
    return jnp.minimum(index * quarter_size(rows), rows - quarter_size(rows))


def padded(weights):
    return jnp.pad(weights, ((0, -weights.shape[0] % 16), (0, 0)))


def own_quarter(weights):
    place = lax.axis_index("req") % 4
    size = quarter_size(weights.shape[0])
    return lax.dynamic_slice_in_dim(weights, quarter_start(weights.shape[0], place), size, 0)


def other_copy(values, flip):
    return lax.ppermute(values, "req", [(i, i ^ flip) for i in range(lax.axis_size("req"))])


def line_neighbours(values, tp_size):
    lines = tp_size // 2
    if lines != 4:
        return [turned(values, tp_size, k) for k in range(1, lines)]
    up = lax.ppermute(values, "tp", [(i, i + 2) for i in range(tp_size - 2)])
    down = lax.ppermute(values, "tp", [(i + 2, i) for i in range(tp_size - 2)])
    return [up, turned(values, tp_size, 2), down]


def line_ends(parts, tp_size, queue):
    if tp_size // 2 != 4:
        return parts
    line = lax.axis_index("tp") // 2
    ends = lax.ppermute(queue.held(parts[1]), "tp", [(2, 0), (3, 1), (4, 6), (5, 7)])
    return [jnp.where(line == 0, ends, parts[0]), parts[1], jnp.where(line == 3, ends, parts[2])]


def shards(
    patches, vis_gain, w_fc1, w_fc2, merge_gain, w_merge, slots, text, docs, dec_gain, w_qkv, w_out
):
    patch_rows = patches[0]
    text_rows = text[0]
    width = patch_rows.shape[1]
    seq_here = text_rows.shape[0]
    tp_size = lax.axis_size("tp")
    lines = tp_size // 2
    line = lax.axis_index("tp") // 2
    side = lax.axis_index("tp") % 2

    blk = 2 * seq_here
    longest = seq_here * tp_size // 4
    halo = -(-longest // blk)
    ahead = halo * blk
    window = ahead + blk
    qkv_own = padded(w_qkv.T)
    out_own = padded(w_out)
    columns, depth = qkv_own.shape[0], out_own.shape[0]
    place = lax.axis_index("req") % 4
    starts = jnp.stack(
        [quarter_start(columns, place ^ i) for i in (0, 1, 2, 3)]
        + [quarter_start(depth, place ^ i) for i in (0, 1, 2, 3)]
        + [line * blk - ahead, side, (2 * line + side) * seq_here, line]
    ).astype(jnp.int32)
    bf16 = jnp.bfloat16

    images = slots.shape[1] // IMG_ROWS
    span = seq_here * tp_size // images
    tables = []
    for target in range(lines):
        held = []
        for place_of in range(images):
            low = place_of * span if place_of < images - 1 else images * span - IMG_ROWS
            inside = low < (target + 1) * blk and (place_of + 1) * span > target * blk - ahead
            held.append((not inside, (place_of - images // 2) % images))
        tables.append(sorted(held))
    needed = max(sum(not outside for outside, _ in held) for held in tables)
    table = jnp.array([[image for _, image in held[:needed]] for held in tables], jnp.int32)
    turned_table = table[(line + jnp.arange(lines)) % lines]
    starts = jnp.concatenate([starts, turned_table.reshape(-1)])
    count = needed * IMG_ROWS
    queue = Queue()
    rounds = [k for k in range(1, lines) if k != lines // 2]
    middle = lines // 2
    other, sums, part = {}, {}, {}

    def run_mlp(k, mine):
        own, given = mlp(queue.held(mine), other[k], vis_gain, w_fc1, w_fc2)
        queue.passed((own, given))
        part[k] = own
        return swap_pair(given, tp_size)

    def add_pair(k, got):
        pair = (queue.held(part[k]).astype(jnp.float32) + got.astype(jnp.float32)).astype(bf16)
        queue.passed(pair)
        return turned(pair, tp_size, lines - k)

    swapping = swap_pair(patch_rows, tp_size)
    moving = {k: turned(patch_rows, tp_size, k) for k in rounds + [middle]}
    text_other = swap_pair(text_rows, tp_size)
    qkv_quarter, out_quarter = queue.passed((own_quarter(qkv_own), own_quarter(out_own)))
    other[0] = queue.wait(swapping)
    mine, swapping = {}, {}
    for k in rounds + [middle]:
        mine[k] = queue.wait(moving[k])
    text_other = queue.wait(text_other)
    for k in rounds + [middle]:
        swapping[k] = swap_pair(queue.held(mine[k]), tp_size)
    qkv_moving, qkv_ours, qkv_theirs = {}, {}, {}
    place_of = {0: 0, middle: lines - 1, **{k: i + 1 for i, k in enumerate(rounds)}}

    def move_weights(k, part=0, parts=1):
        size = qkv_quarter.shape[0] // parts
        piece = qkv_quarter[part * size : (part + 1) * size]
        qkv_moving.setdefault(k, []).append(turned(queue.held(piece), tp_size, k))

    def cross_weights(k):
        halves = queue.wait(qkv_moving[k])
        qkv_moving[k] = halves[0] if len(halves) == 1 else jnp.concatenate(queue.held(halves))
        qkv_theirs[k] = other_copy(queue.held(qkv_moving[k]), 2)

    def share_weights(k):
        both = jnp.stack([queue.held(qkv_moving[k]), queue.wait(qkv_theirs[k])])
        qkv_ours[k] = queue.passed(both[:, None])
        qkv_theirs[k] = other_copy(qkv_ours[k], 1)

    text_back = []
    for steps_back in range(1, halo + 1):
        steps = [(i, i + 2 * steps_back) for i in range(tp_size - 2 * steps_back)]
        text_back.append(lax.ppermute(queue.held(text_rows), "tp", steps))
    back = {0: run_mlp(0, patch_rows)}
    for index, k in enumerate(rounds):
        other[k] = queue.wait(swapping[k])
        if index == 1:
            text_back = queue.wait(text_back)
            move_weights(middle, 0, 2)
        back[k] = run_mlp(k, mine[k])
    other[middle] = queue.wait(swapping[middle])
    back[middle] = run_mlp(middle, mine[middle])
    queue.wait(qkv_moving[middle][0])
    for k in rounds:
        sums[k] = add_pair(k, queue.wait(back[k]))
    got = queue.wait(back[middle])
    for k in rounds:
        queue.wait(sums[k])
    sums[middle] = add_pair(middle, got)
    move_weights(middle, 1, 2)
    pieces = []
    for rows in text_back[::-1]:
        pieces += [rows, swap_pair(queue.held(rows), tp_size)]
    spread, hits, bias, slots_here = queue.passed(kernel_call(
        functools.partial(mask_kernel, blk, longest), "masks",
        [
            ((count, window), bf16),
            ((8, window), jnp.float32),
            ((blk // 128, longest + 128, 128), jnp.float32),
            ((8, count), jnp.int32),
        ],
        starts, queue.held(slots), docs,
    ))
    sums[0] = part[0]
    sums = [queue.wait(back[0])] + [queue.wait(sums[k]) for k in range(lines)]
    cross_weights(middle)
    kept, given = queue.passed(
        spread_rows(starts, queue.held(patch_rows), sums, merge_gain, lines)
    )
    got = swap_pair(queue.held(given), tp_size)
    move_weights(rounds[0])
    pieces = queue.wait(pieces) + [text_rows, text_other]
    text_normed, text_parts = queue.passed(kernel_call(
        text_kernel, "text_first", [((window, width), bf16), ((lines, columns, window), bf16)],
        starts, queue.held(dec_gain), qkv_own, *pieces,
        grid=(1,),
        out_specs=[
            whole_block((window, width)),
            pl.BlockSpec((1, columns, window), lambda _: (0, 0, 0)),
        ],
    ))

    def run_text(text_parts, k):
        return queue.passed(kernel_call(
            text_next_kernel, "text_next", [((lines, columns, window), bf16)],
            starts, queue.held(text_normed), qkv_ours[k], queue.wait(qkv_theirs[k]), text_parts,
            grid=(window // 256,),
            specs={
                1: pl.BlockSpec((256, width), lambda i: (i, 0)),
                4: pl.BlockSpec(memory_space=pl.ANY),
            },
            out_specs=[pl.BlockSpec((1, columns, 256), lambda i: (place_of[k], 0, i))],
            scratch=[pltpu.VMEM((columns, width), bf16)],
            aliases={4: 0},
        ))[0]

    got = queue.wait(got)
    cross_weights(rounds[0])
    share_weights(middle)
    blocks = queue.passed([jnp.concatenate([queue.held(kept[k]), got[k]]) for k in range(lines)])
    blocks = [blocks[0]] + [turned(blocks[k], tp_size, k) for k in range(1, lines)]
    queue.wait(blocks)
    kept, given = queue.passed(merge(starts, [queue.held(blocks[0])] + blocks[1:], w_merge))
    half = kept.shape[1]
    got = swap_pair(given, tp_size)
    for k in rounds[1:]:
        move_weights(k)
    text_parts = run_text(text_parts, middle)
    got = queue.wait(got)
    share = queue.passed(kernel_call(
        functools.partial(split_kernel, needed), "image_shares", [((count, half), bf16)] * lines,
        starts, queue.held(kept), got,
    ))
    moving = [turned(share[k], tp_size, k) for k in range(1, lines)]
    for k in rounds[1:]:
        cross_weights(k)
    share_weights(rounds[0])
    text_parts = run_text(text_parts, rounds[0])
    total = queue.held(share[0]).astype(jnp.float32)
    for block in queue.wait(moving):
        total = total + block.astype(jnp.float32)
    total = queue.passed(total.astype(bf16))
    for k in rounds[1:]:
        share_weights(k)
    far = swap_pair(queue.held(total), tp_size)
    out_moving = [turned(queue.held(out_quarter), tp_size, k) for k in rounds + [middle]]
    for k in rounds[1:]:
        text_parts = run_text(text_parts, k)
    merged, image_rows = queue.passed(kernel_call(
        image_rows_kernel, "image_rows", [((count, width), bf16)] * 2,
        starts, queue.held(total), queue.wait(far), dec_gain,
    ))
    line_pieces = [x[k] for k in rounds + [middle] for x in (qkv_ours, qkv_theirs)]
    sources = [text_parts, qkv_own] + line_pieces
    out_near = queue.passed(jnp.stack(queue.wait([queue.held(part) for part in out_moving])))
    out_far = other_copy(out_near, 2)
    out_beside = other_copy(out_near, 1)
    kept, given = queue.passed(kernel_call(
        functools.partial(late_kernel, blk, longest, lines, depth), "late_attention",
        [((seq_here, lines * depth), bf16)] * 2,
        starts, queue.held(image_rows), spread, hits, bias, *sources,
        specs={5 + i: pl.BlockSpec(memory_space=pl.ANY) for i in range(2 * lines)},
        scratch=[pltpu.VMEM(source.shape, bf16) for source in sources] + [
            pltpu.VMEM((columns, width), bf16),
            pltpu.VMEM((lines * depth, blk), jnp.float32),
            pltpu.SemaphoreType.DMA((3 * lines,)),
        ],
        room=44,
    ))
    out_far = queue.wait(out_far)
    out_across = other_copy(queue.held(out_far), 1)
    quarters = [out_near, queue.wait(out_beside), out_far, queue.wait(out_across)]
    (given,) = queue.passed(project(starts, queue.held(given), out_own, quarters))
    got = swap_pair(given, tp_size)
    (kept,) = queue.passed(project(starts, queue.held(kept), out_own, quarters))
    (own_rows,) = queue.passed(kernel_call(
        out_kernel, "out_rows", [((seq_here, width), jnp.float32)],
        starts, queue.held(text_rows), slots_here, merged, kept,
    ))
    decoded = (queue.held(own_rows) + queue.wait(got).astype(jnp.float32)).astype(bf16)
    return decoded[None]


def solution(mesh):
    placed = (
        P("req", "tp", None),
        P(),
        P(None, "tp"),
        P("tp", None),
        P(),
        P("tp", None),
        P("req", None),
        P("req", "tp", None),
        P("req", None),
        P(),
        P(None, "tp"),
        P("tp", None),
    )
    return jax.shard_map(
        shards, mesh=mesh, in_specs=placed, out_specs=P("req", "tp", None), check_vma=False
    )
```
